512 devices in a mesh: group: 16 (over z, core), dev: 32 (over x, y).
Axes of the slice: x: 4, y: 8, z: 8, core: 2. Of those that a mesh axis runs over, the one named last changes fastest.
Arguments:
- tile_values: bfloat16 [8192, 128, 128], P(('group', 'dev')), may hold values from -0.25 to 0.25
- tile_rows: int32 [8192], P(('group', 'dev')), may hold values from 0 to 1
- tile_columns: int32 [8192], P(('group', 'dev')), may hold values from 0 to 63
- tile_count: int32 [512], P(('group', 'dev')), may hold values from 4 to 16, as said below
- start_basis: bfloat16 [131072, 64], P(('group', 'dev')), may hold values from -6 to 6
- seed_rows: int32 [1024], replicated, may hold values from 0 to 131071
Outputs:
- unit_embedding: float32 [131072, 64], P(('group', 'dev'))
- centroids: float32 [1024, 64], replicated
The draws below stay inside these ranges and needn't reach their ends.
Inputs may be any that keep to these rules, and one draw needn't show every extreme that they name: `tile_count`: the most, 16, is reached by some device in every draw.
All inputs are finite; a program needn't handle non-finite values.
Results may differ from the reference program's by a relative error of at most 0.0029.
Values may be sent and summed in bfloat16 or wider, within the bound.
No kernel may reach another device: no remote copies, remote signals or barrier semaphores. Data moves between devices by JAX's collectives and lax.ppermute only.
A program may use at most 64 MiB of HBM per device.

```python
import jax
import jax.numpy as jnp
from jax import lax

BLOCK = 128
BASIS = 64
CLUSTERS = 1024
ROWS_DEV = 256
TILES_MAX = 16
ITERS = 2
KSTEPS = 2
ROW_BLOCKS = 2
GROUP_BLOCKS = 64
NROWS = 131072
N_GROUP = 16
N_DEV = 32
DEVICES = 512


def draw_tile_count(key, part):
    first_key, second_key, third_key = jax.random.split(jax.random.fold_in(key, 17), 3)
    device_total = N_GROUP * N_DEV
    base = jax.random.randint(first_key, (device_total,), TILES_MAX // 4, TILES_MAX // 2 + 1)
    full = jax.random.randint(second_key, (device_total,), 0, 8) == 0
    counts = jnp.where(full, TILES_MAX, base)
    chosen = jax.random.randint(third_key, (), 0, device_total)
    return counts.at[chosen].set(TILES_MAX).astype(jnp.int32)


def touch_ends(array, key, smallest, top_value):
    place = [jax.random.randint(jax.random.fold_in(key, axis), (), 0, length) for axis, length in enumerate(array.shape)]
    main_axis = array.shape.index(max(array.shape))
    beside = place[:main_axis] + [(place[main_axis] + 1) % array.shape[main_axis]] + place[main_axis + 1:]
    return array.at[tuple(place)].set(smallest).at[tuple(beside)].set(top_value)


def block_scale(stream_key, shape, cuts, least, top_value):
    factor_of = 1.0
    for dim, blocks in cuts:
        draws = jax.random.uniform(jax.random.fold_in(jax.random.fold_in(stream_key, 6), dim), (blocks,), jnp.float32, least / len(cuts), top_value / len(cuts))
        factor_of = factor_of * jnp.repeat(jnp.exp(draws), shape[dim] // blocks).reshape((-1,) + (1,) * (len(shape) - 1 - dim))
    return factor_of


def gaussian(rng, shape, width, most, pieces=(), kind=jnp.bfloat16):
    array = jax.random.normal(rng, shape, jnp.float32) * width
    if len(pieces) > 0:
        array = block_scale(rng, shape, pieces, -0.22, 0.18) * array
    return jnp.clip(array, min=-most, max=most).astype(kind)


def setup_inputs(seed: int = 0) -> dict:
    arg_keys = jax.random.split(jax.random.key(seed), 7)
    tile_values = gaussian(arg_keys[0], (DEVICES * TILES_MAX, BLOCK, BLOCK), (4 * BLOCK) ** -0.5, 0.25, ((0, 512),))
    tile_rows = touch_ends(jax.random.randint(arg_keys[1], (DEVICES * TILES_MAX,), 0, ROW_BLOCKS), jax.random.fold_in(arg_keys[1], 1), 0, ROW_BLOCKS - 1).astype(jnp.int32)
    tile_columns = touch_ends(jax.random.randint(arg_keys[2], (DEVICES * TILES_MAX,), 0, GROUP_BLOCKS), jax.random.fold_in(arg_keys[2], 1), 0, GROUP_BLOCKS - 1).astype(jnp.int32)
    tile_count = draw_tile_count(jax.random.fold_in(arg_keys[6], 71), 0)
    start_basis = gaussian(arg_keys[4], (NROWS, BASIS), 1.0, 6.0, ((0, 512),))
    seed_rows = touch_ends(jax.random.randint(arg_keys[5], (CLUSTERS,), 0, NROWS), jax.random.fold_in(arg_keys[5], 1), 0, NROWS - 1).astype(jnp.int32)
    return {"tile_values": tile_values, "tile_rows": tile_rows, "tile_columns": tile_columns, "tile_count": tile_count, "start_basis": start_basis, "seed_rows": seed_rows}


def apply_tiles(tile_block, row_index, column_index, live_count, group_basis):
    basis_blocks = group_basis.reshape(-1, BLOCK, BASIS)
    picked = jnp.take(basis_blocks, column_index, axis=0)
    products = jnp.einsum('tij,tjk->tik', tile_block.astype(jnp.float32), picked.astype(jnp.float32))
    live = jnp.arange(TILES_MAX, dtype=jnp.int32) < live_count
    block_index = jnp.arange(ROWS_DEV // BLOCK, dtype=jnp.int32)
    select = ((row_index[None, :] == block_index[:, None]) & live[None, :]).astype(jnp.float32)
    total = jnp.einsum('rt,tik->rik', select, products)
    return total.reshape(ROWS_DEV, BASIS)

def reference(tile_values, tile_rows, tile_columns, tile_count, start_basis, seed_rows):
    device_total = N_GROUP * N_DEV
    tiles_each = tile_values.reshape(device_total, TILES_MAX, BLOCK, BLOCK)
    rows_each = tile_rows.reshape(device_total, TILES_MAX)
    columns_each = tile_columns.reshape(device_total, TILES_MAX)
    basis = start_basis
    embedding = None
    for step_index in range(ITERS):
        group_basis = basis.reshape(N_GROUP, N_DEV * ROWS_DEV, BASIS)

        def one_device(device):
            return apply_tiles(tiles_each[device], rows_each[device], columns_each[device], tile_count[device], group_basis[device // N_DEV])
        image = lax.map(one_device, jnp.arange(device_total, dtype=jnp.int32)).reshape(NROWS, BASIS)
        gram = jnp.dot(image.T, image, precision=lax.Precision.HIGHEST)
        lower = jnp.linalg.cholesky(gram)
        solved = lax.linalg.triangular_solve(lower, image, left_side=False, lower=True, transpose_a=True)
        if step_index + 1 < ITERS:
            basis = solved.astype(jnp.bfloat16)
        else:
            embedding = solved * jnp.sqrt(jnp.float32(NROWS))
    unit = embedding / jnp.sqrt(lax.optimization_barrier(jnp.sum(embedding * embedding, axis=1, keepdims=True)) + 1e-06)
    centres = unit[seed_rows]
    unit_blocks = unit.reshape(-1, ROWS_DEV, BASIS)
    for kstep in range(KSTEPS):
        centre_square = lax.optimization_barrier(jnp.sum(centres * centres, axis=1))

        def accumulate(carry, rows_block):
            weighted, mass = carry
            dist = lax.optimization_barrier(jnp.sum(rows_block * rows_block, axis=1))[:, None] - 2.0 * jnp.dot(rows_block, centres.T, precision=lax.Precision.HIGHEST) + centre_square[None, :]
            weights = jnp.exp(-4.0 * dist)
            member = weights / lax.optimization_barrier(jnp.sum(weights, axis=1, keepdims=True))
            weighted = weighted + jnp.dot(member.T, rows_block, precision=lax.Precision.HIGHEST)
            mass = mass + lax.optimization_barrier(jnp.sum(member, axis=0))
            return ((weighted, mass), None)
        start = (jnp.zeros((CLUSTERS, BASIS), jnp.float32), jnp.zeros((CLUSTERS,), jnp.float32))
        (weighted, mass), unused = lax.scan(accumulate, start, unit_blocks)
        centres = weighted / mass[:, None]
    return (unit, centres)
```

```python
import functools

import jax
import jax.numpy as jnp
from jax import lax
from jax.experimental import pallas as pl
from jax.experimental.pallas import tpu as pltpu
from jax.sharding import PartitionSpec as P

KSTEPS = 2
HI = lax.Precision.HIGHEST
F32 = jnp.float32
BF16 = jnp.bfloat16
ALL = ("z", "c", "x", "y")
GROUP = ("z", "c")
DEV = ("x", "y")
LANES = 128
PART = 48
EXTRA = 16
GROW = 2.0**30

sharpness = 4.0


def dot(a, b, dims, precision=None):
    return lax.dot_general(a, b, (dims, ((), ())), precision=precision, preferred_element_type=F32)


def halves(x):
    high = x.astype(BF16)
    return high, (x - high.astype(F32)).astype(BF16)


def tn(a, b):
    ah, al = halves(a)
    bh, bl = halves(b)
    return dot(jnp.concatenate([ah, ah, al], axis=0), jnp.concatenate([bh, bl, bh], axis=0), ((0,), (0,)))


def nn_exact(a, b):
    ah, al = halves(a)
    both = dot(jnp.concatenate([ah, al], axis=0), b, ((1,), (0,)))
    return both[: a.shape[0]] + both[a.shape[0] :]


def inverse_cholesky(gram):
    n = gram.shape[0]
    blocks = n // 8
    width = 2 * n
    lane = lax.broadcasted_iota(jnp.int32, (8, n), 1)
    sub = lax.broadcasted_iota(jnp.int32, (8, n), 0)
    wide_sub = lax.broadcasted_iota(jnp.int32, (8, width), 0)
    rows = [
        jnp.concatenate([gram[8 * b : 8 * b + 8, :], (lane == sub + 8 * b).astype(F32)], axis=1)
        for b in range(blocks)
    ]
    for g in range(blocks):
        columns = [
            {b: jnp.broadcast_to(rows[b][:, 8 * g + t : 8 * g + t + 1], (8, width)) for b in range(g, blocks)}
            for t in range(8)
        ]
        pivots = jnp.ones((8, width), F32)
        for t in range(8):
            pivot = jnp.broadcast_to(columns[t][g][t : t + 1, :], (8, width))
            pivots = jnp.where(wide_sub == t, pivot, pivots)
            inverse = 1.0 / pivot
            row = jnp.broadcast_to(rows[g][t : t + 1, :], (8, width))
            later = {m: jnp.broadcast_to(columns[m][g][t : t + 1, :], (8, width)) for m in range(t + 1, 8)}
            for b in range(g, blocks):
                factor = columns[t][b] * inverse
                if b == g:
                    factor = jnp.where(wide_sub > t, factor, 0.0)
                rows[b] = rows[b] - factor * row
                for m in range(t + 1, 8):
                    columns[m][b] = columns[m][b] - factor * later[m]
        rows[g] = rows[g] / jnp.sqrt(pivots)
    return jnp.concatenate(rows, axis=0)[:, n:]


def apply_tiles(count, rows, columns, tiles, gathered):
    slots, block, _ = tiles.shape
    width = gathered.shape[1]
    row_blocks = gathered.shape[2] // block
    total = [jnp.zeros((width, block), F32) for _ in range(row_blocks)]
    for s in range(slots):
        place = columns[s]
        start = pl.multiple_of((place % row_blocks) * block, block)
        picked = gathered[place // row_blocks, :, pl.ds(start, block)]
        product = dot(picked, tiles[s], ((1,), (1,)))
        live = s < count[0]
        for r in range(row_blocks):
            total[r] = total[r] + jnp.where(live & (rows[s] == r), product, 0.0)
    return jnp.concatenate(total, axis=1)


def store_pieces(out, features, extra):
    both = jnp.concatenate([features, extra], axis=0)
    for k in range(features.shape[1] // LANES):
        tile = both[:, k * LANES : (k + 1) * LANES].astype(out.dtype)
        out[2 * k] = tile[:PART]
        rest = tile[PART:]
        pad = jnp.zeros((2 * PART - both.shape[0], LANES), out.dtype)
        out[2 * k + 1] = jnp.concatenate([rest, pad], axis=0)


def load_pieces(pieces, width):
    features, extra = [], []
    for k in range(pieces.shape[0] // 2):
        low, high = pieces[2 * k].astype(F32), pieces[2 * k + 1].astype(F32)
        features.append(jnp.concatenate([low, high[: width - PART]], axis=0))
        extra.append(high[width - PART : width - PART + EXTRA])
    return features, extra


def first_kernel(count, rows, columns, tiles, gathered, spread, gram):
    image = apply_tiles(count, rows, columns, tiles, gathered)
    gram[...] = dot(image, image, ((1,), (1,)), HI)
    narrow = image.astype(BF16)
    for e in range(spread.shape[0]):
        spread[e] = narrow


def second_kernel(count, rows, columns, first, tiles, gathered, gram, seeds, image_out, pieces):
    image = apply_tiles(count, rows, columns, tiles, gathered) * GROW
    image_out[...] = image
    second = dot(image, image, ((1,), (1,)), HI)
    node = lax.broadcasted_iota(jnp.int32, (image.shape[1], seeds.shape[1]), 0)
    chooser = jnp.where(seeds[...] - first[0] == node, 1.0, 0.0).astype(BF16)
    picks = nn_exact(image, chooser)
    grams = jnp.concatenate([gram[...], second], axis=1)
    tiles_of_clusters = seeds.shape[1] // LANES
    each = grams.shape[0] // tiles_of_clusters
    extra = jnp.concatenate([grams[k * each : (k + 1) * each] for k in range(tiles_of_clusters)], axis=1)
    extra = jnp.concatenate([extra, jnp.zeros((EXTRA - each, extra.shape[1]), F32)], axis=0)
    store_pieces(pieces, picks, extra)


def unit_of(transform, image, total_rows):
    embedding = tn(transform, image) * jnp.sqrt(F32(total_rows))
    return embedding / jnp.sqrt(jnp.sum(embedding * embedding, axis=0, keepdims=True) + 1e-06)


def with_rows(top, first, second):
    sub = lax.broadcasted_iota(jnp.int32, (EXTRA, top.shape[1]), 0)
    return jnp.concatenate([top, jnp.where(sub == 0, first, jnp.where(sub == 1, second, 0.0))], axis=0)


def store_sums(pieces, unit, centres):
    width = unit.shape[0]
    square = jnp.sum(unit * unit, axis=0, keepdims=True)
    centre_square = jnp.sum(centres * centres, axis=0, keepdims=True)
    dist = tn(with_rows(unit, square, 1.0), with_rows(-2.0 * centres, 1.0, centre_square))
    weights = jnp.exp(-sharpness * dist)
    member = (weights / jnp.sum(weights, axis=1, keepdims=True)).astype(BF16)
    sums = nn_exact(with_rows(unit, 1.0, 0.0), member)
    store_pieces(pieces, sums[:width], sums[width:])


def third_kernel(image, received, unit_out, pieces, *, total_rows):
    width = image.shape[0]
    picks, grams = load_pieces(received, width)
    each = width // len(grams)
    grams = jnp.concatenate([g[:each] for g in grams], axis=0)
    inverse = inverse_cholesky(grams[:, :width])
    second = dot(dot(inverse, grams[:, width:], ((1,), (0,)), HI), inverse, ((1,), (1,)), HI)
    again = inverse_cholesky(second)
    transform = dot(inverse, again, ((0,), (1,)), HI)
    unit = unit_of(transform, image[...], total_rows)
    unit_out[...] = unit
    store_sums(pieces, unit, unit_of(transform, jnp.concatenate(picks, axis=1), total_rows))


def centres_of(received, width):
    sums, extra = load_pieces(received, width)
    return jnp.concatenate([s / e[:1] for s, e in zip(sums, extra)], axis=1)


def fourth_kernel(unit, received, pieces):
    store_sums(pieces, unit[...], centres_of(received, unit.shape[0]))


def last_kernel(received, centres):
    centres[...] = centres_of(received, centres.shape[0])


def fold_kernel(received, spread):
    total = received[0].astype(F32)
    for e in range(1, received.shape[0]):
        total = total + received[e].astype(F32)
    total = total.astype(spread.dtype)
    for e in range(spread.shape[0]):
        spread[e] = total


VMEM = pl.BlockSpec(memory_space=pltpu.VMEM)
SMEM = pl.BlockSpec(memory_space=pltpu.SMEM)


def call(kernel, specs, outs, *args):
    return pl.pallas_call(
        kernel,
        in_specs=specs,
        out_specs=[VMEM] * len(outs),
        out_shape=[jax.ShapeDtypeStruct(s, d) for s, d in outs],
        compiler_params=pltpu.CompilerParams(vmem_limit_bytes=40 * 1024 * 1024),
    )(*args)


def exchange(x, axes):
    return lax.all_to_all(x, axes, 0, 0, tiled=True)


def fold(x, copies, dtype):
    return call(fold_kernel, [VMEM], [((copies,) + x.shape[1:], dtype)], x)[0]


def sum_pieces(pieces, middle, last):
    mine = fold(exchange(pieces, GROUP), lax.axis_size(DEV), middle)
    return exchange(fold(exchange(mine, DEV), pieces.shape[0], last), GROUP)


def local(tile_values, tile_rows, tile_columns, tile_count, start_basis, seed_rows):
    local_rows, width = start_basis.shape
    clusters = seed_rows.shape[0]
    total_rows = local_rows * lax.axis_size(ALL)
    first = jnp.reshape(lax.axis_index(ALL) * local_rows, (1,)).astype(jnp.int32)
    group = (lax.axis_size(DEV), width, local_rows)
    pieces = (lax.axis_size(GROUP), PART, LANES)

    gathered = exchange(jnp.broadcast_to(start_basis.T[None], group), DEV)
    spread, gram = call(
        first_kernel,
        [SMEM, SMEM, SMEM, VMEM, VMEM],
        [(group, BF16), ((width, width), F32)],
        tile_count, tile_rows, tile_columns, tile_values, gathered,
    )
    gathered = exchange(spread, DEV)
    image, sums = call(
        second_kernel,
        [SMEM, SMEM, SMEM, SMEM, VMEM, VMEM, VMEM, VMEM],
        [((width, local_rows), F32), (pieces, F32)],
        tile_count, tile_rows, tile_columns, first, tile_values, gathered, gram, seed_rows[None, :],
    )
    sums = sum_pieces(sums, F32, F32)
    unit, sums = call(
        functools.partial(third_kernel, total_rows=total_rows),
        [VMEM] * 2,
        [((width, local_rows), F32), (pieces, F32)],
        image, sums,
    )
    for _ in range(KSTEPS - 1):
        sums = sum_pieces(sums, F32, F32)
        (sums,) = call(fourth_kernel, [VMEM] * 2, [(pieces, F32)], unit, sums)
    sums = sum_pieces(sums, F32, F32)
    (centres,) = call(last_kernel, [VMEM], [((width, clusters), F32)], sums)
    return unit.T, centres.T


def solution(mesh):
    sizes = (mesh.shape["group"] // 2, 2, mesh.shape["dev"] // 8, 8)
    fine = jax.sharding.Mesh(mesh.devices.reshape(sizes), ALL)
    return jax.shard_map(
        local,
        mesh=fine,
        in_specs=(P(ALL, None, None), P(ALL), P(ALL), P(ALL), P(ALL, None), P()),
        out_specs=(P(ALL, None), P()),
        check_vma=False,
    )
```

```python
import functools

import jax
import jax.numpy as jnp
from jax import lax
from jax.experimental import pallas as pl
from jax.experimental.pallas import tpu as pltpu
from jax.sharding import PartitionSpec as P

KSTEPS = 2
HI = lax.Precision.HIGHEST
F32 = jnp.float32
BF16 = jnp.bfloat16
ALL = ("z", "c", "x", "y")
GROUP = ("z", "c")
DEV = ("x", "y")
LANES = 128
PART = 16
EXTRA = 8
GROW = 2.0**30

sharpness = 4.0


def dot(a, b, dims, precision=None):
    return lax.dot_general(a, b, (dims, ((), ())), precision=precision, preferred_element_type=F32)


def halves(x):
    high = x.astype(BF16)
    return high, (x - high.astype(F32)).astype(BF16)


def tn(a, b):
    ah, al = halves(a)
    bh, bl = halves(b)
    return dot(jnp.concatenate([ah, ah, al], axis=0), jnp.concatenate([bh, bl, bh], axis=0), ((0,), (0,)))


def nn_exact(a, b):
    ah, al = halves(a)
    both = dot(jnp.concatenate([ah, al], axis=0), b, ((1,), (0,)))
    return both[: a.shape[0]] + both[a.shape[0] :]


def inverse_cholesky(gram):
    n = gram.shape[0]
    blocks = n // 8
    width = 2 * n
    lane = lax.broadcasted_iota(jnp.int32, (8, n), 1)
    sub = lax.broadcasted_iota(jnp.int32, (8, n), 0)
    wide_sub = lax.broadcasted_iota(jnp.int32, (8, width), 0)
    rows = [
        jnp.concatenate([gram[8 * b : 8 * b + 8, :], (lane == sub + 8 * b).astype(F32)], axis=1)
        for b in range(blocks)
    ]
    for g in range(blocks):
        columns = [
            {b: jnp.broadcast_to(rows[b][:, 8 * g + t : 8 * g + t + 1], (8, width)) for b in range(g, blocks)}
            for t in range(8)
        ]
        pivots = jnp.ones((8, width), F32)
        for t in range(8):
            pivot = jnp.broadcast_to(columns[t][g][t : t + 1, :], (8, width))
            pivots = jnp.where(wide_sub == t, pivot, pivots)
            inverse = 1.0 / pivot
            row = jnp.broadcast_to(rows[g][t : t + 1, :], (8, width))
            later = {m: jnp.broadcast_to(columns[m][g][t : t + 1, :], (8, width)) for m in range(t + 1, 8)}
            for b in range(g, blocks):
                factor = columns[t][b] * inverse
                if b == g:
                    factor = jnp.where(wide_sub > t, factor, 0.0)
                rows[b] = rows[b] - factor * row
                for m in range(t + 1, 8):
                    columns[m][b] = columns[m][b] - factor * later[m]
        rows[g] = rows[g] / jnp.sqrt(pivots)
    return jnp.concatenate(rows, axis=0)[:, n:]


def apply_tiles(count, rows, columns, tiles, gathered):
    slots, block, _ = tiles.shape
    width = gathered.shape[1]
    row_blocks = gathered.shape[2] // block
    total = [jnp.zeros((width, block), F32) for _ in range(row_blocks)]
    for s in range(slots):
        place = columns[s]
        start = pl.multiple_of((place % row_blocks) * block, block)
        picked = gathered[place // row_blocks, :, pl.ds(start, block)]
        product = dot(picked, tiles[s], ((1,), (1,)))
        live = s < count[0]
        for r in range(row_blocks):
            total[r] = total[r] + jnp.where(live & (rows[s] == r), product, 0.0)
    return jnp.concatenate(total, axis=1)


def store_pieces(out, features, blocks):
    for k in range(features.shape[1] // LANES):
        for q in range(features.shape[0] // PART):
            p = k * (features.shape[0] // PART) + q
            tile = features[q * PART : (q + 1) * PART, k * LANES : (k + 1) * LANES]
            out[p] = jnp.concatenate([tile, blocks[p]], axis=0).astype(out.dtype)


def load_features(pieces, width):
    each = width // PART
    tiles = [
        jnp.concatenate([pieces[k * each + q, :PART] for q in range(each)], axis=0)
        for k in range(pieces.shape[0] // each)
    ]
    return jnp.concatenate(tiles, axis=1)


def first_kernel(count, rows, columns, tiles, gathered, spread, gram):
    image = apply_tiles(count, rows, columns, tiles, gathered)
    gram[...] = dot(image, image, ((1,), (1,)), HI)
    narrow = image.astype(BF16)
    for e in range(spread.shape[0]):
        spread[e] = narrow


def second_kernel(count, rows, columns, first, tiles, gathered, gram, seeds, image_out, pieces):
    image = apply_tiles(count, rows, columns, tiles, gathered) * GROW
    image_out[...] = image
    second = dot(image, image, ((1,), (1,)), HI)
    node = lax.broadcasted_iota(jnp.int32, (image.shape[1], seeds.shape[1]), 0)
    chooser = jnp.where(seeds[...] - first[0] == node, 1.0, 0.0).astype(BF16)
    picks = nn_exact(image, chooser)
    grams = jnp.concatenate([gram[...], second], axis=1)
    empty = jnp.zeros((EXTRA, LANES), F32)
    used = grams.shape[0] // EXTRA
    blocks = [grams[p * EXTRA : (p + 1) * EXTRA] if p < used else empty for p in range(pieces.shape[0])]
    store_pieces(pieces, picks, blocks)


def unit_of(transform, image, total_rows):
    embedding = tn(transform, image) * jnp.sqrt(F32(total_rows))
    return embedding / jnp.sqrt(jnp.sum(embedding * embedding, axis=0, keepdims=True) + 1e-06)


def with_rows(top, first, second):
    sub = lax.broadcasted_iota(jnp.int32, (2 * EXTRA, top.shape[1]), 0)
    return jnp.concatenate([top, jnp.where(sub == 0, first, jnp.where(sub == 1, second, 0.0))], axis=0)


def store_sums(pieces, unit, centres):
    width = unit.shape[0]
    square = jnp.sum(unit * unit, axis=0, keepdims=True)
    centre_square = jnp.sum(centres * centres, axis=0, keepdims=True)
    dist = tn(with_rows(unit, square, 1.0), with_rows(-2.0 * centres, 1.0, centre_square))
    weights = jnp.exp(-sharpness * dist)
    member = (weights / jnp.sum(weights, axis=1, keepdims=True)).astype(BF16)
    sums = nn_exact(with_rows(unit, 1.0, 0.0), member)
    each = width // PART
    blocks = [
        sums[width : width + EXTRA, (p // each) * LANES : (p // each + 1) * LANES] for p in range(pieces.shape[0])
    ]
    store_pieces(pieces, sums[:width], blocks)


def third_kernel(image, received, unit_out, pieces, *, total_rows):
    width = image.shape[0]
    grams = jnp.concatenate([received[p, PART : PART + EXTRA] for p in range(width // EXTRA)], axis=0)
    inverse = inverse_cholesky(grams[:, :width])
    second = dot(dot(inverse, grams[:, width:], ((1,), (0,)), HI), inverse, ((1,), (1,)), HI)
    again = inverse_cholesky(second)
    transform = dot(inverse, again, ((0,), (1,)), HI)
    unit = unit_of(transform, image[...], total_rows)
    unit_out[...] = unit
    store_sums(pieces, unit, unit_of(transform, load_features(received, width), total_rows))


def fourth_kernel(unit, received, pieces):
    store_sums(pieces, unit[...], load_features(received, unit.shape[0]))


def last_kernel(received, centres):
    centres[...] = load_features(received, centres.shape[0])


def total_of(received):
    total = received[0].astype(F32)
    for e in range(1, received.shape[0]):
        total = total + received[e].astype(F32)
    return total


def fold_kernel(received, spread):
    total = total_of(received).astype(spread.dtype)
    for e in range(spread.shape[0]):
        spread[e] = total


def mean_kernel(received, spread):
    total = total_of(received)
    total = total[:PART] / total[PART : PART + 1]
    for e in range(spread.shape[0]):
        spread[e] = total


VMEM = pl.BlockSpec(memory_space=pltpu.VMEM)
SMEM = pl.BlockSpec(memory_space=pltpu.SMEM)


def call(kernel, specs, outs, *args):
    return pl.pallas_call(
        kernel,
        in_specs=specs,
        out_specs=[VMEM] * len(outs),
        out_shape=[jax.ShapeDtypeStruct(s, d) for s, d in outs],
        compiler_params=pltpu.CompilerParams(vmem_limit_bytes=40 * 1024 * 1024),
    )(*args)


def exchange(x, axes):
    return lax.all_to_all(x, axes, 0, 0, tiled=True)


def fold(kernel, x, copies, rows, dtype):
    return call(kernel, [VMEM], [((copies, rows, LANES), dtype)], x)[0]


def sum_pieces(pieces, kernel, rows):
    mine = fold(fold_kernel, exchange(pieces, DEV), lax.axis_size(GROUP), pieces.shape[1], pieces.dtype)
    return exchange(fold(kernel, exchange(mine, GROUP), pieces.shape[0], rows, F32), DEV)


def local(tile_values, tile_rows, tile_columns, tile_count, start_basis, seed_rows):
    local_rows, width = start_basis.shape
    clusters = seed_rows.shape[0]
    total_rows = local_rows * lax.axis_size(ALL)
    first = jnp.reshape(lax.axis_index(ALL) * local_rows, (1,)).astype(jnp.int32)
    seeds = seed_rows[None, :]
    group = (lax.axis_size(DEV), width, local_rows)
    pieces = (lax.axis_size(DEV), PART + EXTRA, LANES)

    spread = jnp.broadcast_to(start_basis.T[None], group)
    spread, first, seeds, tile_rows, tile_columns, tile_count = lax.optimization_barrier(
        (spread, first, seeds, tile_rows, tile_columns, tile_count)
    )
    gathered = exchange(spread, DEV)
    spread, gram = call(
        first_kernel,
        [SMEM, SMEM, SMEM, VMEM, VMEM],
        [(group, BF16), ((width, width), F32)],
        tile_count, tile_rows, tile_columns, tile_values, gathered,
    )
    gathered = exchange(spread, DEV)
    image, sums = call(
        second_kernel,
        [SMEM, SMEM, SMEM, SMEM, VMEM, VMEM, VMEM, VMEM],
        [((width, local_rows), F32), (pieces, F32)],
        tile_count, tile_rows, tile_columns, first, tile_values, gathered, gram, seeds,
    )
    sums = sum_pieces(sums, fold_kernel, PART + EXTRA)
    unit, sums = call(
        functools.partial(third_kernel, total_rows=total_rows),
        [VMEM] * 2,
        [((width, local_rows), F32), (pieces, BF16)],
        image, sums,
    )
    for _ in range(KSTEPS - 1):
        centres = sum_pieces(sums, mean_kernel, PART)
        (sums,) = call(fourth_kernel, [VMEM] * 2, [(pieces, BF16)], unit, centres)
    centres = sum_pieces(sums, mean_kernel, PART)
    (centres,) = call(last_kernel, [VMEM], [((width, clusters), F32)], centres)
    return unit.T, centres.T


def solution(mesh):
    sizes = (mesh.shape["group"] // 2, 2, mesh.shape["dev"] // 8, 8)
    fine = jax.sharding.Mesh(mesh.devices.reshape(sizes), ALL)
    return jax.shard_map(
        local,
        mesh=fine,
        in_specs=(P(ALL, None, None), P(ALL), P(ALL), P(ALL), P(ALL, None), P()),
        out_specs=(P(ALL, None), P()),
        check_vma=False,
    )
```

```python
import functools

import jax
import jax.numpy as jnp
from jax import lax
from jax.experimental import pallas as pl
from jax.experimental.pallas import tpu as pltpu
from jax.sharding import PartitionSpec as P

KSTEPS = 2
HI = lax.Precision.HIGHEST
F32 = jnp.float32
BF16 = jnp.bfloat16
ALL = ("z", "c", "x", "y")
GROUP = ("z", "c")
DEV = ("x", "y")
LANES = 128
PART = 16
EXTRA = 2
ROWS = PART + EXTRA
GROW = 2.0**30

sharpness = 4.0


def dot(a, b, dims, precision=None):
    return lax.dot_general(a, b, (dims, ((), ())), precision=precision, preferred_element_type=F32)


def halves(x):
    high = x.astype(BF16)
    return high, (x - high.astype(F32)).astype(BF16)


def tn(a, b):
    ah, al = halves(a)
    bh, bl = halves(b)
    return dot(jnp.concatenate([ah, ah, al], axis=0), jnp.concatenate([bh, bl, bh], axis=0), ((0,), (0,)))


def nn_exact(a, b):
    ah, al = halves(a)
    both = dot(jnp.concatenate([ah, al], axis=0), b, ((1,), (0,)))
    return both[: a.shape[0]] + both[a.shape[0] :]


def inverse_cholesky(gram):
    n = gram.shape[0]
    blocks = n // 8
    width = 2 * n
    lane = lax.broadcasted_iota(jnp.int32, (8, n), 1)
    sub = lax.broadcasted_iota(jnp.int32, (8, n), 0)
    wide_sub = lax.broadcasted_iota(jnp.int32, (8, width), 0)
    rows = [
        jnp.concatenate([gram[8 * b : 8 * b + 8, :], (lane == sub + 8 * b).astype(F32)], axis=1)
        for b in range(blocks)
    ]
    for g in range(blocks):
        columns = [
            {b: jnp.broadcast_to(rows[b][:, 8 * g + t : 8 * g + t + 1], (8, width)) for b in range(g, blocks)}
            for t in range(8)
        ]
        pivots = jnp.ones((8, width), F32)
        for t in range(8):
            pivot = jnp.broadcast_to(columns[t][g][t : t + 1, :], (8, width))
            pivots = jnp.where(wide_sub == t, pivot, pivots)
            inverse = 1.0 / pivot
            row = jnp.broadcast_to(rows[g][t : t + 1, :], (8, width))
            later = {m: jnp.broadcast_to(columns[m][g][t : t + 1, :], (8, width)) for m in range(t + 1, 8)}
            for b in range(g, blocks):
                factor = columns[t][b] * inverse
                if b == g:
                    factor = jnp.where(wide_sub > t, factor, 0.0)
                rows[b] = rows[b] - factor * row
                for m in range(t + 1, 8):
                    columns[m][b] = columns[m][b] - factor * later[m]
        rows[g] = rows[g] / jnp.sqrt(pivots)
    return jnp.concatenate(rows, axis=0)[:, n:]


def apply_tiles(count, rows, columns, tiles, gathered):
    slots, block, _ = tiles.shape
    width = gathered.shape[1]
    row_blocks = gathered.shape[2] // block
    total = [jnp.zeros((width, block), F32) for _ in range(row_blocks)]
    for s in range(slots):
        place = columns[s]
        start = pl.multiple_of((place % row_blocks) * block, block)
        picked = gathered[place // row_blocks, :, pl.ds(start, block)]
        product = dot(picked, tiles[s], ((1,), (1,)))
        live = s < count[0]
        for r in range(row_blocks):
            total[r] = total[r] + jnp.where(live & (rows[s] == r), product, 0.0)
    return jnp.concatenate(total, axis=1)


def store_pieces(out, features, blocks):
    each = features.shape[0] // PART
    pieces = [
        piece
        for p in range(each * features.shape[1] // LANES)
        for piece in (
            features[(p % each) * PART : (p % each + 1) * PART, (p // each) * LANES : (p // each + 1) * LANES],
            blocks[p],
        )
    ]
    out[...] = jnp.concatenate(pieces, axis=0).astype(out.dtype)


def load_features(pieces, width):
    each = width // PART
    tiles = [
        jnp.concatenate([pieces[k * each + q] for q in range(each)], axis=0) for k in range(len(pieces) // each)
    ]
    return jnp.concatenate(tiles, axis=1)


def cut(array, rows):
    return [array[p : p + rows] for p in range(0, array.shape[0], rows)]


def first_kernel(count, rows, columns, tiles, gathered, spread, gram):
    image = apply_tiles(count, rows, columns, tiles, gathered)
    gram[...] = dot(image, image, ((1,), (1,)), HI)
    narrow = image.astype(BF16)
    for e in range(spread.shape[0]):
        spread[e] = narrow


def second_kernel(count, rows, columns, first, tiles, gathered, gram, seeds, image_out, pieces):
    image = apply_tiles(count, rows, columns, tiles, gathered) * GROW
    image_out[...] = image
    second = dot(image, image, ((1,), (1,)), HI)
    node = lax.broadcasted_iota(jnp.int32, (image.shape[1], seeds.shape[1]), 0)
    chooser = jnp.where(seeds[...] - first[0] == node, 1.0, 0.0).astype(BF16)
    picks = nn_exact(image, chooser)
    grams = jnp.concatenate([gram[...], second], axis=1)
    store_pieces(pieces, picks, cut(grams, EXTRA))


def unit_of(transform, image, total_rows):
    embedding = tn(transform, image) * jnp.sqrt(F32(total_rows))
    return embedding / jnp.sqrt(jnp.sum(embedding * embedding, axis=0, keepdims=True) + 1e-06)


def with_rows(top, first, second):
    sub = lax.broadcasted_iota(jnp.int32, (16, top.shape[1]), 0)
    return jnp.concatenate([top, jnp.where(sub == 0, first, jnp.where(sub == 1, second, 0.0))], axis=0)


def store_sums(pieces, unit, centres):
    width = unit.shape[0]
    square = jnp.sum(unit * unit, axis=0, keepdims=True)
    centre_square = jnp.sum(centres * centres, axis=0, keepdims=True)
    dist = tn(with_rows(unit, square, 1.0), with_rows(-2.0 * centres, 1.0, centre_square))
    weights = jnp.exp(-sharpness * dist)
    member = (weights / jnp.sum(weights, axis=1, keepdims=True)).astype(BF16)
    sums = nn_exact(with_rows(unit, 1.0, 0.0), member)
    each = width // PART
    blocks = [
        sums[width : width + EXTRA, (p // each) * LANES : (p // each + 1) * LANES] for p in range(pieces.shape[0] // ROWS)
    ]
    store_pieces(pieces, sums[:width], blocks)


def third_kernel(image, received, unit_out, pieces, *, total_rows):
    width = image.shape[0]
    parts = cut(received[...], ROWS)
    grams = jnp.concatenate([part[PART:] for part in parts], axis=0)
    inverse = inverse_cholesky(grams[:, :width])
    second = dot(dot(inverse, grams[:, width:], ((1,), (0,)), HI), inverse, ((1,), (1,)), HI)
    again = inverse_cholesky(second)
    transform = dot(inverse, again, ((0,), (1,)), HI)
    unit = unit_of(transform, image[...], total_rows)
    unit_out[...] = unit
    picks = load_features([part[:PART] for part in parts], width)
    store_sums(pieces, unit, unit_of(transform, picks, total_rows))


def fourth_kernel(unit, received, pieces):
    store_sums(pieces, unit[...], load_features(cut(received[...], PART), unit.shape[0]))


def last_kernel(received, centres):
    centres[...] = load_features(cut(received[...], PART), centres.shape[0])


def fold_kernel(received, spread):
    total = sum(cut(received[...].astype(F32), ROWS)).astype(spread.dtype)
    spread[...] = jnp.concatenate([total] * (spread.shape[0] // ROWS), axis=0)


def mean_kernel(received, spread):
    total = sum(cut(received[...].astype(F32), ROWS))
    total = total[:PART] / total[PART : PART + 1]
    spread[...] = jnp.concatenate([total] * (spread.shape[0] // PART), axis=0)


VMEM = pl.BlockSpec(memory_space=pltpu.VMEM)
SMEM = pl.BlockSpec(memory_space=pltpu.SMEM)


def call(kernel, specs, outs, *args):
    return pl.pallas_call(
        kernel,
        in_specs=specs,
        out_specs=[VMEM] * len(outs),
        out_shape=[jax.ShapeDtypeStruct(s, d) for s, d in outs],
        compiler_params=pltpu.CompilerParams(vmem_limit_bytes=40 * 1024 * 1024),
    )(*args)


def exchange(x, axes):
    return lax.all_to_all(x, axes, 0, 0, tiled=True)


def exchange_rows(x, axes):
    together = 4 // x.dtype.itemsize
    return exchange(x.reshape(-1, together, LANES), axes).reshape(x.shape)


def gather_group(spread):
    part = exchange(spread, ("y",))
    whole = exchange(jnp.broadcast_to(part[None], (lax.axis_size("x"),) + part.shape), ("x",))
    return whole.reshape((-1,) + part.shape[1:])


def fold(kernel, x, rows, dtype):
    return call(kernel, [VMEM], [((rows, LANES), dtype)], x)[0]


def sum_pieces(pieces, middle, kernel, rows):
    mine = fold(fold_kernel, exchange_rows(pieces, DEV), ROWS * lax.axis_size(GROUP), middle)
    return exchange_rows(fold(kernel, exchange_rows(mine, GROUP), rows * lax.axis_size(DEV), F32), DEV)


def local(tile_values, tile_rows, tile_columns, tile_count, start_basis, seed_rows):
    local_rows, width = start_basis.shape
    clusters = seed_rows.shape[0]
    total_rows = local_rows * lax.axis_size(ALL)
    first = jnp.reshape(lax.axis_index(ALL) * local_rows, (1,)).astype(jnp.int32)
    seeds = seed_rows[None, :]
    group = (lax.axis_size("y"), width, local_rows)
    pieces = (lax.axis_size(DEV) * ROWS, LANES)

    spread = jnp.broadcast_to(start_basis.T[None], group)
    spread, first, seeds, tile_rows, tile_columns, tile_count = lax.optimization_barrier(
        (spread, first, seeds, tile_rows, tile_columns, tile_count)
    )
    gathered = gather_group(spread)
    spread, gram = call(
        first_kernel,
        [SMEM, SMEM, SMEM, VMEM, VMEM],
        [(group, BF16), ((width, width), F32)],
        tile_count, tile_rows, tile_columns, tile_values, gathered,
    )
    gathered = gather_group(spread)
    image, sums = call(
        second_kernel,
        [SMEM, SMEM, SMEM, SMEM, VMEM, VMEM, VMEM, VMEM],
        [((width, local_rows), F32), (pieces, F32)],
        tile_count, tile_rows, tile_columns, first, tile_values, gathered, gram, seeds,
    )
    sums = sum_pieces(sums, F32, fold_kernel, ROWS)
    unit, sums = call(
        functools.partial(third_kernel, total_rows=total_rows),
        [VMEM] * 2,
        [((width, local_rows), F32), (pieces, BF16)],
        image, sums,
    )
    for _ in range(KSTEPS - 1):
        centres = sum_pieces(sums, F32, mean_kernel, PART)
        (sums,) = call(fourth_kernel, [VMEM] * 2, [(pieces, BF16)], unit, centres)
    centres = sum_pieces(sums, F32, mean_kernel, PART)
    (centres,) = call(last_kernel, [VMEM], [((width, clusters), F32)], centres)
    return unit.T, centres.T


def solution(mesh):
    sizes = (mesh.shape["group"] // 2, 2, mesh.shape["dev"] // 8, 8)
    fine = jax.sharding.Mesh(mesh.devices.reshape(sizes), ALL)
    return jax.shard_map(
        local,
        mesh=fine,
        in_specs=(P(ALL, None, None), P(ALL), P(ALL), P(ALL), P(ALL, None), P()),
        out_specs=(P(ALL, None), P()),
        check_vma=False,
    )
```

```python
import functools

import jax
import jax.numpy as jnp
from jax import lax
from jax.experimental import pallas as pl
from jax.experimental.pallas import tpu as pltpu
from jax.sharding import PartitionSpec as P

KSTEPS = 2
HI = lax.Precision.HIGHEST
F32 = jnp.float32
BF16 = jnp.bfloat16
ALL = ("z", "c", "x", "y")
GROUP = ("z",)
CHIP = "c"
DEV = ("x", "y")
LANES = 128
PART = 8
EXTRA = 2
ROWS = PART + EXTRA
GROW = 2.0**30

sharpness = 4.0


def dot(a, b, dims, precision=None):
    return lax.dot_general(a, b, (dims, ((), ())), precision=precision, preferred_element_type=F32)


def halves(x):
    high = x.astype(BF16)
    return high, (x - high.astype(F32)).astype(BF16)


def tn(a, b):
    ah, al = halves(a)
    bh, bl = halves(b)
    return dot(jnp.concatenate([ah, ah, al], axis=0), jnp.concatenate([bh, bl, bh], axis=0), ((0,), (0,)))


def nn_exact(a, b):
    ah, al = halves(a)
    both = dot(jnp.concatenate([ah, al], axis=0), b, ((1,), (0,)))
    return both[: a.shape[0]] + both[a.shape[0] :]


def inverse_cholesky(gram):
    n = gram.shape[0]
    blocks = n // 8
    width = 2 * n
    lane = lax.broadcasted_iota(jnp.int32, (8, n), 1)
    sub = lax.broadcasted_iota(jnp.int32, (8, n), 0)
    wide_sub = lax.broadcasted_iota(jnp.int32, (8, width), 0)
    rows = [
        jnp.concatenate([gram[8 * b : 8 * b + 8, :], (lane == sub + 8 * b).astype(F32)], axis=1)
        for b in range(blocks)
    ]
    for g in range(blocks):
        columns = [
            {b: jnp.broadcast_to(rows[b][:, 8 * g + t : 8 * g + t + 1], (8, width)) for b in range(g, blocks)}
            for t in range(8)
        ]
        pivots = jnp.ones((8, width), F32)
        for t in range(8):
            pivot = jnp.broadcast_to(columns[t][g][t : t + 1, :], (8, width))
            pivots = jnp.where(wide_sub == t, pivot, pivots)
            inverse = 1.0 / pivot
            row = jnp.broadcast_to(rows[g][t : t + 1, :], (8, width))
            later = {m: jnp.broadcast_to(columns[m][g][t : t + 1, :], (8, width)) for m in range(t + 1, 8)}
            for b in range(g, blocks):
                factor = columns[t][b] * inverse
                if b == g:
                    factor = jnp.where(wide_sub > t, factor, 0.0)
                rows[b] = rows[b] - factor * row
                for m in range(t + 1, 8):
                    columns[m][b] = columns[m][b] - factor * later[m]
        rows[g] = rows[g] / jnp.sqrt(pivots)
    return jnp.concatenate(rows, axis=0)[:, n:]


def apply_tiles(count, rows, columns, tiles, gathered):
    slots, block, _ = tiles.shape
    width = gathered.shape[1]
    row_blocks = gathered.shape[2] // block
    total = [jnp.zeros((width, block), F32) for _ in range(row_blocks)]
    for s in range(slots):
        place = columns[s]
        start = pl.multiple_of((place % row_blocks) * block, block)
        picked = gathered[place // row_blocks, :, pl.ds(start, block)]
        product = dot(picked, tiles[s], ((1,), (1,)))
        live = s < count[...]
        for r in range(row_blocks):
            total[r] = total[r] + jnp.where(live & (rows[s] == r), product, 0.0)
    return jnp.concatenate(total, axis=1)


def store_pieces(out, features, blocks):
    each = features.shape[0] // PART
    pieces = [
        piece
        for p in range(each * features.shape[1] // LANES)
        for piece in (
            features[(p % each) * PART : (p % each + 1) * PART, (p // each) * LANES : (p // each + 1) * LANES],
            blocks[p],
        )
    ]
    out[...] = jnp.concatenate(pieces, axis=0).astype(out.dtype)


def load_features(pieces, width):
    each = width // PART
    tiles = [
        jnp.concatenate([pieces[k * each + q] for q in range(each)], axis=0) for k in range(len(pieces) // each)
    ]
    return jnp.concatenate(tiles, axis=1)


def cut(array, rows):
    return [array[p : p + rows] for p in range(0, array.shape[0], rows)]


def first_kernel(rows, columns, count, tiles, gathered, spread, gram):
    image = apply_tiles(count, rows, columns, tiles, gathered)
    gram[...] = dot(image, image, ((1,), (1,)), HI)
    narrow = image.astype(BF16)
    for e in range(spread.shape[0]):
        spread[e] = narrow


def second_kernel(rows, columns, count, tiles, gathered, gram, own):
    image = apply_tiles(count, rows, columns, tiles, gathered) * GROW
    nodes = image.shape[1]
    own[:, :nodes] = image
    own[:, nodes:] = jnp.concatenate([gram[...], dot(image, image, ((1,), (1,)), HI)], axis=1)


def pick_kernel(first, seeds, both, pieces, *, nodes, apart):
    node = lax.broadcasted_iota(jnp.int32, (nodes, seeds.shape[1]), 0) + first[0]
    picks = sum(
        nn_exact(both[c, :, :nodes], jnp.where(seeds[...] == node + c * apart, 1.0, 0.0).astype(BF16))
        for c in range(both.shape[0])
    )
    store_pieces(pieces, picks, cut(sum(both[c, :, nodes:] for c in range(both.shape[0])), EXTRA))


def unit_of(transform, image, total_rows):
    embedding = tn(transform, image) * jnp.sqrt(F32(total_rows))
    return embedding / jnp.sqrt(jnp.sum(embedding * embedding, axis=0, keepdims=True) + 1e-06)


def with_rows(top, first, second):
    sub = lax.broadcasted_iota(jnp.int32, (16, top.shape[1]), 0)
    return jnp.concatenate([top, jnp.where(sub == 0, first, jnp.where(sub == 1, second, 0.0))], axis=0)


def store_weights(weights, sums, unit, centres):
    square = jnp.sum(unit * unit, axis=0, keepdims=True)
    centre_square = jnp.sum(centres * centres, axis=0, keepdims=True)
    dist = tn(with_rows(-2.0 * centres, 1.0, centre_square), with_rows(unit, square, 1.0))
    value = jnp.exp(-sharpness * dist)
    weights[...] = value
    sums[...] = jnp.sum(value, axis=0, keepdims=True)


def third_kernel(own, both, received, unit_own, unit_both, weights, sums, *, total_rows):
    width, nodes = unit_own.shape
    parts = cut(received[...], ROWS)
    grams = jnp.concatenate([part[PART:] for part in parts], axis=0)
    inverse = inverse_cholesky(grams[:, :width])
    second = dot(dot(inverse, grams[:, width:], ((1,), (0,)), HI), inverse, ((1,), (1,)), HI)
    again = inverse_cholesky(second)
    transform = dot(inverse, again, ((0,), (1,)), HI)
    unit_own[...] = unit_of(transform, own[:, :nodes], total_rows)
    images = jnp.concatenate([both[c, :, :nodes] for c in range(both.shape[0])], axis=1)
    unit = unit_of(transform, images, total_rows)
    unit_both[...] = unit
    picks = load_features([part[:PART] for part in parts], width)
    store_weights(weights, sums, unit, unit_of(transform, picks, total_rows))


def weight_kernel(unit, received, weights, sums):
    store_weights(weights, sums, unit[...], load_features(cut(received[...], PART), unit.shape[0]))


def sum_kernel(unit, weights, sums, pieces):
    width = unit.shape[0]
    member = (weights[...] / sum(sums[c] for c in range(sums.shape[0]))).astype(BF16)
    high, low = halves(with_rows(unit[...], 1.0, 0.0))
    both = dot(jnp.concatenate([high, low], axis=0), member, ((1,), (1,)))
    total = both[: high.shape[0]] + both[high.shape[0] :]
    each = width // PART
    blocks = [
        total[width : width + EXTRA, (p // each) * LANES : (p // each + 1) * LANES]
        for p in range(pieces.shape[0] // ROWS)
    ]
    store_pieces(pieces, total[:width], blocks)


def last_kernel(received, centres):
    halves_of = [load_features(cut(received[c], PART), centres.shape[0]) for c in range(received.shape[0])]
    centres[...] = jnp.concatenate(halves_of, axis=1)


def fold_kernel(received, spread):
    total = sum(cut(received[...].astype(F32), ROWS)).astype(spread.dtype)
    spread[...] = jnp.concatenate([total] * (spread.shape[0] // ROWS), axis=0)


def mean_kernel(received, spread):
    total = sum(cut(received[...].astype(F32), ROWS))
    total = total[:PART] / total[PART : PART + 1]
    spread[...] = jnp.concatenate([total] * (spread.shape[0] // PART), axis=0)


VMEM = pl.BlockSpec(memory_space=pltpu.VMEM)
SMEM = pl.BlockSpec(memory_space=pltpu.SMEM)


def call(kernel, specs, outs, *args):
    return pl.pallas_call(
        kernel,
        in_specs=specs,
        out_specs=[VMEM] * len(outs),
        out_shape=[jax.ShapeDtypeStruct(s, d) for s, d in outs],
        compiler_params=pltpu.CompilerParams(vmem_limit_bytes=40 * 1024 * 1024),
    )(*args)


def exchange(x, axes):
    return lax.all_to_all(x, axes, 0, 0, tiled=True)


def exchange_rows(x, axes):
    together = 4 // x.dtype.itemsize
    return exchange(x.reshape(-1, together, LANES), axes).reshape(x.shape)


def gather_group(spread):
    part = exchange(spread, ("y",))
    whole = exchange(jnp.broadcast_to(part[None], (lax.axis_size("x"),) + part.shape), ("x",))
    return whole.reshape((-1,) + part.shape[1:])


def fold(kernel, x, rows, dtype):
    return call(kernel, [VMEM], [((rows, LANES), dtype)], x)[0]


def sum_pieces(pieces, middle, kernel, rows):
    mine = fold(fold_kernel, exchange_rows(pieces, DEV), ROWS * lax.axis_size(GROUP), middle)
    return exchange_rows(fold(kernel, exchange_rows(mine, GROUP), rows * lax.axis_size(DEV), F32), DEV)


def of_chip(x):
    return lax.all_gather(x, CHIP, axis=0)


def local(tile_values, tile_rows, tile_columns, tile_count, start_basis, seed_rows):
    local_rows, width = start_basis.shape
    cores, devices = lax.axis_size(CHIP), lax.axis_size(DEV)
    clusters = seed_rows.shape[0]
    mine = clusters // cores
    nodes = cores * local_rows
    total_rows = local_rows * lax.axis_size(ALL)
    apart = devices * local_rows
    first = lax.axis_index("z") * (cores * apart) + lax.axis_index(DEV) * local_rows
    first = jnp.reshape(first, (1,)).astype(jnp.int32)
    seeds = lax.dynamic_slice_in_dim(seed_rows, lax.axis_index(CHIP) * mine, mine, 0)[None, :]
    count = tile_count[None, :]
    group = (lax.axis_size("y"), width, local_rows)
    pieces = (devices * ROWS, LANES)

    spread = jnp.broadcast_to(start_basis.T[None], group)
    spread, first, seeds, tile_rows, tile_columns, count = lax.optimization_barrier(
        (spread, first, seeds, tile_rows, tile_columns, count)
    )
    gathered = gather_group(spread)
    spread, gram = call(
        first_kernel,
        [SMEM, SMEM, VMEM, VMEM, VMEM],
        [(group, BF16), ((width, width), F32)],
        tile_rows, tile_columns, count, tile_values, gathered,
    )
    gathered = gather_group(spread)
    (own,) = call(
        second_kernel,
        [SMEM, SMEM, VMEM, VMEM, VMEM, VMEM],
        [((width, local_rows + 2 * width), F32)],
        tile_rows, tile_columns, count, tile_values, gathered, gram,
    )
    both = of_chip(own)
    (sums,) = call(
        functools.partial(pick_kernel, nodes=local_rows, apart=apart),
        [SMEM, VMEM, VMEM],
        [(pieces, F32)],
        first, seeds, both,
    )
    sums = sum_pieces(sums, F32, fold_kernel, ROWS)
    unit, unit_both, weights, totals = call(
        functools.partial(third_kernel, total_rows=total_rows),
        [VMEM] * 3,
        [((width, local_rows), F32), ((width, nodes), F32), ((mine, nodes), F32), ((1, nodes), F32)],
        own, both, sums,
    )
    for step in range(KSTEPS):
        if step > 0:
            weights, totals = call(
                weight_kernel, [VMEM] * 2, [((mine, nodes), F32), ((1, nodes), F32)], unit_both, centres
            )
        (sums,) = call(sum_kernel, [VMEM] * 3, [(pieces, BF16)], unit_both, weights, of_chip(totals))
        centres = sum_pieces(sums, F32, mean_kernel, PART)
    (centres,) = call(last_kernel, [VMEM], [((width, clusters), F32)], of_chip(centres))
    return unit.T, centres.T


def solution(mesh):
    sizes = (mesh.shape["group"] // 2, 2, mesh.shape["dev"] // 8, 8)
    fine = jax.sharding.Mesh(mesh.devices.reshape(sizes), ALL)
    return jax.shard_map(
        local,
        mesh=fine,
        in_specs=(P(ALL, None, None), P(ALL), P(ALL), P(ALL), P(ALL, None), P()),
        out_specs=(P(ALL, None), P()),
        check_vma=False,
    )
```

```python
import functools

import jax
import jax.numpy as jnp
from jax import lax
from jax.experimental import pallas as pl
from jax.experimental.pallas import tpu as pltpu
from jax.sharding import PartitionSpec as P

KSTEPS = 2
HI = lax.Precision.HIGHEST
F32 = jnp.float32
BF16 = jnp.bfloat16
ALL = ("z", "c", "x", "y")
GROUP = ("z",)
CHIP = "c"
DEV = ("x", "y")
LANES = 128
PART = 8
EXTRA = 2
ROWS = PART + EXTRA
GROW = 2.0**30

sharpness = 4.0


def dot(a, b, dims, precision=None):
    return lax.dot_general(a, b, (dims, ((), ())), precision=precision, preferred_element_type=F32)


def halves(x):
    high = x.astype(BF16)
    return high, (x - high.astype(F32)).astype(BF16)


def tn(a, b):
    ah, al = halves(a)
    bh, bl = halves(b)
    return dot(jnp.concatenate([ah, ah, al], axis=0), jnp.concatenate([bh, bl, bh], axis=0), ((0,), (0,)))


def nn_exact(a, b):
    ah, al = halves(a)
    both = dot(jnp.concatenate([ah, al], axis=0), b, ((1,), (0,)))
    return both[: a.shape[0]] + both[a.shape[0] :]


def inverse_cholesky(gram):
    n = gram.shape[0]
    blocks = n // 8
    width = 2 * n
    lane = lax.broadcasted_iota(jnp.int32, (8, n), 1)
    sub = lax.broadcasted_iota(jnp.int32, (8, n), 0)
    wide_sub = lax.broadcasted_iota(jnp.int32, (8, width), 0)
    rows = [
        jnp.concatenate([gram[8 * b : 8 * b + 8, :], (lane == sub + 8 * b).astype(F32)], axis=1)
        for b in range(blocks)
    ]
    for g in range(blocks):
        columns = [
            {b: jnp.broadcast_to(rows[b][:, 8 * g + t : 8 * g + t + 1], (8, width)) for b in range(g, blocks)}
            for t in range(8)
        ]
        pivots = jnp.ones((8, width), F32)
        for t in range(8):
            pivot = jnp.broadcast_to(columns[t][g][t : t + 1, :], (8, width))
            pivots = jnp.where(wide_sub == t, pivot, pivots)
            inverse = 1.0 / pivot
            row = jnp.broadcast_to(rows[g][t : t + 1, :], (8, width))
            later = {m: jnp.broadcast_to(columns[m][g][t : t + 1, :], (8, width)) for m in range(t + 1, 8)}
            for b in range(g, blocks):
                factor = columns[t][b] * inverse
                if b == g:
                    factor = jnp.where(wide_sub > t, factor, 0.0)
                rows[b] = rows[b] - factor * row
                for m in range(t + 1, 8):
                    columns[m][b] = columns[m][b] - factor * later[m]
        rows[g] = rows[g] / jnp.sqrt(pivots)
    return jnp.concatenate(rows, axis=0)[:, n:]


def apply_tiles(rows, columns, tiles, gathered):
    slots, block, _ = tiles.shape
    width = gathered.shape[1]
    row_blocks = gathered.shape[2] // block
    total = [jnp.zeros((width, block), F32) for _ in range(row_blocks)]
    for s in range(slots):
        place = columns[s]
        start = pl.multiple_of((place % row_blocks) * block, block)
        picked = gathered[place // row_blocks, :, pl.ds(start, block)]
        product = dot(picked, tiles[s], ((1,), (1,)))
        for r in range(row_blocks):
            total[r] = total[r] + jnp.where(rows[s] == r, product, 0.0)
    return jnp.concatenate(total, axis=1)


def store_pieces(out, features, blocks):
    each = features.shape[0] // PART
    pieces = [
        piece
        for p in range(each * features.shape[1] // LANES)
        for piece in (
            features[(p % each) * PART : (p % each + 1) * PART, (p // each) * LANES : (p // each + 1) * LANES],
            blocks[p],
        )
    ]
    out[...] = jnp.concatenate(pieces, axis=0).astype(out.dtype)


def load_features(pieces, width):
    each = width // PART
    tiles = [
        jnp.concatenate([pieces[k * each + q] for q in range(each)], axis=0) for k in range(len(pieces) // each)
    ]
    return jnp.concatenate(tiles, axis=1)


def cut(array, rows):
    return [array[p : p + rows] for p in range(0, array.shape[0], rows)]


def first_kernel(rows, columns, tiles, gathered, spread, gram):
    image = apply_tiles(rows, columns, tiles, gathered)
    gram[...] = dot(image, image, ((1,), (1,)), HI)
    narrow = image.astype(BF16)
    for e in range(spread.shape[0]):
        spread[e] = narrow


def second_kernel(rows, columns, tiles, gathered, gram, own):
    image = apply_tiles(rows, columns, tiles, gathered) * GROW
    nodes = image.shape[1]
    own[:, :nodes] = image
    own[:, nodes:] = jnp.concatenate([gram[...], dot(image, image, ((1,), (1,)), HI)], axis=1)


def pick_kernel(first, seeds, both, pieces, *, nodes, apart):
    node = lax.broadcasted_iota(jnp.int32, (nodes, seeds.shape[1]), 0) + first[0]
    picks = sum(
        nn_exact(both[c, :, :nodes], jnp.where(seeds[...] == node + c * apart, 1.0, 0.0).astype(BF16))
        for c in range(both.shape[0])
    )
    store_pieces(pieces, picks, cut(sum(both[c, :, nodes:] for c in range(both.shape[0])), EXTRA))


def unit_of(transform, image, total_rows):
    embedding = tn(transform, image) * jnp.sqrt(F32(total_rows))
    return embedding / jnp.sqrt(jnp.sum(embedding * embedding, axis=0, keepdims=True) + 1e-06)


def with_rows(top, first, second):
    sub = lax.broadcasted_iota(jnp.int32, (16, top.shape[1]), 0)
    return jnp.concatenate([top, jnp.where(sub == 0, first, jnp.where(sub == 1, second, 0.0))], axis=0)


def store_weights(weights, sums, unit, centres):
    square = jnp.sum(unit * unit, axis=0, keepdims=True)
    centre_square = jnp.sum(centres * centres, axis=0, keepdims=True)
    dist = tn(with_rows(-2.0 * centres, 1.0, centre_square), with_rows(unit, square, 1.0))
    value = jnp.exp(-sharpness * dist)
    weights[...] = value
    sums[...] = jnp.sum(value, axis=0, keepdims=True)


def third_kernel(own, both, received, unit_own, unit_both, weights, sums, *, total_rows):
    width, nodes = unit_own.shape
    parts = cut(received[...], ROWS)
    grams = jnp.concatenate([part[PART:] for part in parts], axis=0)
    inverse = inverse_cholesky(grams[:, :width])
    second = dot(dot(inverse, grams[:, width:], ((1,), (0,)), HI), inverse, ((1,), (1,)), HI)
    again = inverse_cholesky(second)
    transform = dot(inverse, again, ((0,), (1,)), HI)
    unit_own[...] = unit_of(transform, own[:, :nodes], total_rows)
    images = jnp.concatenate([both[c, :, :nodes] for c in range(both.shape[0])], axis=1)
    unit = unit_of(transform, images, total_rows)
    unit_both[...] = unit
    picks = load_features([part[:PART] for part in parts], width)
    store_weights(weights, sums, unit, unit_of(transform, picks, total_rows))


def weight_kernel(unit, received, weights, sums):
    store_weights(weights, sums, unit[...], load_features(cut(received[...], PART), unit.shape[0]))


def sum_kernel(unit, weights, sums, pieces):
    width = unit.shape[0]
    member = (weights[...] / sum(sums[c] for c in range(sums.shape[0]))).astype(BF16)
    high, low = halves(with_rows(unit[...], 1.0, 0.0))
    both = dot(jnp.concatenate([high, low], axis=0), member, ((1,), (1,)))
    total = both[: high.shape[0]] + both[high.shape[0] :]
    each = width // PART
    blocks = [
        total[width : width + EXTRA, (p // each) * LANES : (p // each + 1) * LANES]
        for p in range(pieces.shape[0] // ROWS)
    ]
    store_pieces(pieces, total[:width], blocks)


def last_kernel(received, centres):
    halves_of = [load_features(cut(received[c], PART), centres.shape[0]) for c in range(received.shape[0])]
    centres[...] = jnp.concatenate(halves_of, axis=1)


def fold_kernel(received, spread):
    total = sum(cut(received[...].astype(F32), ROWS)).astype(spread.dtype)
    spread[...] = jnp.concatenate([total] * (spread.shape[0] // ROWS), axis=0)


def mean_kernel(received, spread):
    total = sum(cut(received[...].astype(F32), ROWS))
    total = total[:PART] / total[PART : PART + 1]
    spread[...] = jnp.concatenate([total] * (spread.shape[0] // PART), axis=0)


VMEM = pl.BlockSpec(memory_space=pltpu.VMEM)
SMEM = pl.BlockSpec(memory_space=pltpu.SMEM)


def call(kernel, specs, outs, *args):
    return pl.pallas_call(
        kernel,
        in_specs=specs,
        out_specs=[VMEM] * len(outs),
        out_shape=[jax.ShapeDtypeStruct(s, d) for s, d in outs],
        compiler_params=pltpu.CompilerParams(vmem_limit_bytes=40 * 1024 * 1024),
    )(*args)


def exchange(x, axes):
    return lax.all_to_all(x, axes, 0, 0, tiled=True)


def exchange_rows(x, axes):
    together = 4 // x.dtype.itemsize
    return exchange(x.reshape(-1, together, LANES), axes).reshape(x.shape)


def gather_group(spread):
    part = exchange(spread, ("y",))
    whole = exchange(jnp.broadcast_to(part[None], (lax.axis_size("x"),) + part.shape), ("x",))
    return whole.reshape((-1,) + part.shape[1:])


def fold(kernel, x, rows, dtype):
    return call(kernel, [VMEM], [((rows, LANES), dtype)], x)[0]


def sum_pieces(pieces, middle, kernel, rows):
    mine = fold(fold_kernel, exchange_rows(pieces, DEV), ROWS * lax.axis_size(GROUP), middle)
    return exchange_rows(fold(kernel, exchange_rows(mine, GROUP), rows * lax.axis_size(DEV), F32), DEV)


def of_chip(x):
    return lax.all_gather(x, CHIP, axis=0)


def local(tile_values, tile_rows, tile_columns, tile_count, start_basis, seed_rows):
    local_rows, width = start_basis.shape
    cores, devices = lax.axis_size(CHIP), lax.axis_size(DEV)
    clusters = seed_rows.shape[0]
    mine = clusters // cores
    nodes = cores * local_rows
    total_rows = local_rows * lax.axis_size(ALL)
    apart = devices * local_rows
    first = lax.axis_index("z") * (cores * apart) + lax.axis_index(DEV) * local_rows
    first = jnp.reshape(first, (1,)).astype(jnp.int32)
    seeds = lax.dynamic_slice_in_dim(seed_rows, lax.axis_index(CHIP) * mine, mine, 0)[None, :]
    rows = jnp.where(jnp.arange(tile_rows.shape[0], dtype=jnp.int32) < tile_count[0], tile_rows, -1)
    group = (lax.axis_size("y"), width, local_rows)
    pieces = (devices * ROWS, LANES)

    spread = jnp.broadcast_to(start_basis.T[None], group)
    spread, first, seeds, rows = lax.optimization_barrier((spread, first, seeds, rows))
    gathered = gather_group(spread)
    spread, gram = call(
        first_kernel,
        [SMEM, SMEM, VMEM, VMEM],
        [(group, BF16), ((width, width), F32)],
        rows, tile_columns, tile_values, gathered,
    )
    gathered = gather_group(spread)
    (own,) = call(
        second_kernel,
        [SMEM, SMEM, VMEM, VMEM, VMEM],
        [((width, local_rows + 2 * width), F32)],
        rows, tile_columns, tile_values, gathered, gram,
    )
    both = of_chip(own)
    (sums,) = call(
        functools.partial(pick_kernel, nodes=local_rows, apart=apart),
        [SMEM, VMEM, VMEM],
        [(pieces, F32)],
        first, seeds, both,
    )
    sums = sum_pieces(sums, F32, fold_kernel, ROWS)
    unit, unit_both, weights, totals = call(
        functools.partial(third_kernel, total_rows=total_rows),
        [VMEM] * 3,
        [((width, local_rows), F32), ((width, nodes), F32), ((mine, nodes), F32), ((1, nodes), F32)],
        own, both, sums,
    )
    for step in range(KSTEPS):
        if step > 0:
            weights, totals = call(
                weight_kernel, [VMEM] * 2, [((mine, nodes), F32), ((1, nodes), F32)], unit_both, centres
            )
        (sums,) = call(sum_kernel, [VMEM] * 3, [(pieces, BF16)], unit_both, weights, of_chip(totals))
        centres = sum_pieces(sums, F32, mean_kernel, PART)
    (centres,) = call(last_kernel, [VMEM], [((width, clusters), F32)], of_chip(centres))
    return unit.T, centres.T


def solution(mesh):
    sizes = (mesh.shape["group"] // 2, 2, mesh.shape["dev"] // 8, 8)
    fine = jax.sharding.Mesh(mesh.devices.reshape(sizes), ALL)
    return jax.shard_map(
        local,
        mesh=fine,
        in_specs=(P(ALL, None, None), P(ALL), P(ALL), P(ALL), P(ALL, None), P()),
        out_specs=(P(ALL, None), P()),
        check_vma=False,
    )
```

```python
import functools

import jax
import jax.numpy as jnp
from jax import lax
from jax.experimental import pallas as pl
from jax.experimental.pallas import tpu as pltpu
from jax.sharding import PartitionSpec as P

KSTEPS = 2
HI = lax.Precision.HIGHEST
F32 = jnp.float32
BF16 = jnp.bfloat16
ALL = ("z", "c", "x", "y")
GROUP = ("z",)
CHIP = "c"
DEV = ("x", "y")
LANES = 128
PART = 8
EXTRA = 2
ROWS = PART + EXTRA
GROW = 2.0**30

sharpness = 4.0


def dot(a, b, dims, precision=None):
    return lax.dot_general(a, b, (dims, ((), ())), precision=precision, preferred_element_type=F32)


def halves(x):
    high = x.astype(BF16)
    return high, (x - high.astype(F32)).astype(BF16)


def tn(a, b):
    ah, al = halves(a)
    bh, bl = halves(b)
    return dot(jnp.concatenate([ah, ah, al], axis=0), jnp.concatenate([bh, bl, bh], axis=0), ((0,), (0,)))


def nn_exact(a, b):
    ah, al = halves(a)
    both = dot(jnp.concatenate([ah, al], axis=0), b, ((1,), (0,)))
    return both[: a.shape[0]] + both[a.shape[0] :]


def inverse_cholesky(gram):
    n = gram.shape[0]
    blocks = n // 8
    width = 2 * n
    lane = lax.broadcasted_iota(jnp.int32, (8, n), 1)
    sub = lax.broadcasted_iota(jnp.int32, (8, n), 0)
    wide_sub = lax.broadcasted_iota(jnp.int32, (8, width), 0)
    rows = [
        jnp.concatenate([gram[8 * b : 8 * b + 8, :], (lane == sub + 8 * b).astype(F32)], axis=1)
        for b in range(blocks)
    ]
    for g in range(blocks):
        columns = [
            {b: jnp.broadcast_to(rows[b][:, 8 * g + t : 8 * g + t + 1], (8, width)) for b in range(g, blocks)}
            for t in range(8)
        ]
        pivots = jnp.ones((8, width), F32)
        for t in range(8):
            pivot = jnp.broadcast_to(columns[t][g][t : t + 1, :], (8, width))
            pivots = jnp.where(wide_sub == t, pivot, pivots)
            inverse = 1.0 / pivot
            row = jnp.broadcast_to(rows[g][t : t + 1, :], (8, width))
            later = {m: jnp.broadcast_to(columns[m][g][t : t + 1, :], (8, width)) for m in range(t + 1, 8)}
            for b in range(g, blocks):
                factor = columns[t][b] * inverse
                if b == g:
                    factor = jnp.where(wide_sub > t, factor, 0.0)
                rows[b] = rows[b] - factor * row
                for m in range(t + 1, 8):
                    columns[m][b] = columns[m][b] - factor * later[m]
        rows[g] = rows[g] / jnp.sqrt(pivots)
    return jnp.concatenate(rows, axis=0)[:, n:]


def apply_tiles(plan, tiles, gathered):
    slots, block, _ = tiles.shape
    row_blocks = gathered.shape[2] // block
    left = [[] for _ in range(row_blocks)]
    for s in range(slots):
        place = plan[1, s]
        start = pl.multiple_of((place % row_blocks) * block, block)
        picked = gathered[place // row_blocks, :, pl.ds(start, block)]
        for r in range(row_blocks):
            left[r].append(jnp.where(plan[0, s] == r, picked, jnp.zeros_like(picked)))
    left = jnp.concatenate([jnp.concatenate(parts, axis=1) for parts in left], axis=0)
    right = jnp.concatenate([tiles[s] for s in range(slots)], axis=1)
    total = dot(left, right, ((1,), (1,)))
    width = gathered.shape[1]
    return jnp.concatenate([total[r * width : (r + 1) * width] for r in range(row_blocks)], axis=1)


def store_pieces(out, features, blocks):
    each = features.shape[0] // PART
    pieces = [
        piece
        for p in range(each * features.shape[1] // LANES)
        for piece in (
            features[(p % each) * PART : (p % each + 1) * PART, (p // each) * LANES : (p // each + 1) * LANES],
            blocks[p],
        )
    ]
    out[...] = jnp.concatenate(pieces, axis=0).astype(out.dtype)


def load_features(pieces, width):
    each = width // PART
    tiles = [
        jnp.concatenate([pieces[k * each + q] for q in range(each)], axis=0) for k in range(len(pieces) // each)
    ]
    return jnp.concatenate(tiles, axis=1)


def cut(array, rows):
    return [array[p : p + rows] for p in range(0, array.shape[0], rows)]


def first_kernel(plan, tiles, gathered, spread, gram):
    image = apply_tiles(plan, tiles, gathered)
    gram[...] = dot(image, image, ((1,), (1,)), HI)
    narrow = image.astype(BF16)
    for e in range(spread.shape[0]):
        spread[e] = narrow


def second_kernel(plan, tiles, gathered, gram, own):
    image = apply_tiles(plan, tiles, gathered) * GROW
    nodes = image.shape[1]
    own[:, :nodes] = image
    own[:, nodes:] = jnp.concatenate([gram[...], dot(image, image, ((1,), (1,)), HI)], axis=1)


def pick_kernel(first, begin, seeds, both, pieces, *, nodes, apart, clusters):
    chosen = seeds[:, pl.ds(pl.multiple_of(begin[0], LANES), clusters)]
    node = lax.broadcasted_iota(jnp.int32, (nodes, clusters), 0) + first[0]
    picks = sum(
        nn_exact(both[c, :, :nodes], jnp.where(chosen == node + c * apart, 1.0, 0.0).astype(BF16))
        for c in range(both.shape[0])
    )
    store_pieces(pieces, picks, cut(sum(both[c, :, nodes:] for c in range(both.shape[0])), EXTRA))


def unit_of(transform, image, total_rows):
    embedding = tn(transform, image) * jnp.sqrt(F32(total_rows))
    return embedding / jnp.sqrt(jnp.sum(embedding * embedding, axis=0, keepdims=True) + 1e-06)


def with_rows(top, first, second):
    sub = lax.broadcasted_iota(jnp.int32, (16, top.shape[1]), 0)
    return jnp.concatenate([top, jnp.where(sub == 0, first, jnp.where(sub == 1, second, 0.0))], axis=0)


def store_weights(weights, sums, unit, centres):
    square = jnp.sum(unit * unit, axis=0, keepdims=True)
    centre_square = jnp.sum(centres * centres, axis=0, keepdims=True)
    dist = tn(with_rows(-2.0 * centres, 1.0, centre_square), with_rows(unit, square, 1.0))
    value = jnp.exp(-sharpness * dist)
    weights[...] = value
    sums[...] = jnp.sum(value, axis=0, keepdims=True)


def third_kernel(own, both, received, unit_own, unit_both, weights, sums, *, total_rows):
    width, nodes = unit_own.shape
    parts = cut(received[...], ROWS)
    grams = jnp.concatenate([part[PART:] for part in parts], axis=0)
    inverse = inverse_cholesky(grams[:, :width])
    second = dot(dot(inverse, grams[:, width:], ((1,), (0,)), HI), inverse, ((1,), (1,)), HI)
    again = inverse_cholesky(second)
    transform = dot(inverse, again, ((0,), (1,)), HI)
    unit_own[...] = unit_of(transform, own[:, :nodes], total_rows)
    images = jnp.concatenate([both[c, :, :nodes] for c in range(both.shape[0])], axis=1)
    unit = unit_of(transform, images, total_rows)
    unit_both[...] = unit
    picks = load_features([part[:PART] for part in parts], width)
    store_weights(weights, sums, unit, unit_of(transform, picks, total_rows))


def weight_kernel(unit, received, weights, sums):
    store_weights(weights, sums, unit[...], load_features(cut(received[...], PART), unit.shape[0]))


def sum_kernel(unit, weights, sums, pieces):
    width = unit.shape[0]
    member = (weights[...] / sum(sums[c] for c in range(sums.shape[0]))).astype(BF16)
    high, low = halves(with_rows(unit[...], 1.0, 0.0))
    both = dot(jnp.concatenate([high, low], axis=0), member, ((1,), (1,)))
    total = both[: high.shape[0]] + both[high.shape[0] :]
    each = width // PART
    blocks = [
        total[width : width + EXTRA, (p // each) * LANES : (p // each + 1) * LANES]
        for p in range(pieces.shape[0] // ROWS)
    ]
    store_pieces(pieces, total[:width], blocks)


def last_kernel(received, centres):
    halves_of = [load_features(cut(received[c], PART), centres.shape[0]) for c in range(received.shape[0])]
    centres[...] = jnp.concatenate(halves_of, axis=1)


def fold_kernel(received, spread):
    total = sum(cut(received[...].astype(F32), ROWS)).astype(spread.dtype)
    spread[...] = jnp.concatenate([total] * (spread.shape[0] // ROWS), axis=0)


def mean_kernel(received, spread):
    total = sum(cut(received[...].astype(F32), ROWS))
    total = total[:PART] / total[PART : PART + 1]
    spread[...] = jnp.concatenate([total] * (spread.shape[0] // PART), axis=0)


VMEM = pl.BlockSpec(memory_space=pltpu.VMEM)
SMEM = pl.BlockSpec(memory_space=pltpu.SMEM)


def call(kernel, specs, outs, *args):
    return pl.pallas_call(
        kernel,
        in_specs=specs,
        out_specs=[VMEM] * len(outs),
        out_shape=[jax.ShapeDtypeStruct(s, d) for s, d in outs],
        compiler_params=pltpu.CompilerParams(vmem_limit_bytes=40 * 1024 * 1024),
    )(*args)


def exchange(x, axes):
    return lax.all_to_all(x, axes, 0, 0, tiled=True)


def exchange_rows(x, axes):
    together = 4 // x.dtype.itemsize
    return exchange(x.reshape(-1, together, LANES), axes).reshape(x.shape)


def gather_group(spread):
    part = exchange(spread, ("y",))
    whole = exchange(jnp.broadcast_to(part[None], (lax.axis_size("x"),) + part.shape), ("x",))
    return whole.reshape((-1,) + part.shape[1:])


def fold(kernel, x, rows, dtype):
    return call(kernel, [VMEM], [((rows, LANES), dtype)], x)[0]


def sum_pieces(pieces, middle, kernel, rows):
    mine = fold(fold_kernel, exchange_rows(pieces, DEV), ROWS * lax.axis_size(GROUP), middle)
    return exchange_rows(fold(kernel, exchange_rows(mine, GROUP), rows * lax.axis_size(DEV), F32), DEV)


def of_chip(x):
    return lax.all_gather(x, CHIP, axis=0)


def local(tile_values, tile_rows, tile_columns, tile_count, start_basis, seed_rows):
    local_rows, width = start_basis.shape
    cores, devices = lax.axis_size(CHIP), lax.axis_size(DEV)
    clusters = seed_rows.shape[0]
    mine = clusters // cores
    nodes = cores * local_rows
    total_rows = local_rows * lax.axis_size(ALL)
    apart = devices * local_rows
    first = lax.axis_index("z") * (cores * apart) + lax.axis_index(DEV) * local_rows
    first = jnp.reshape(first, (1,)).astype(jnp.int32)
    begin = jnp.reshape(lax.axis_index(CHIP) * mine, (1,)).astype(jnp.int32)
    rows = jnp.where(jnp.arange(tile_rows.shape[0], dtype=jnp.int32) < tile_count[0], tile_rows, -1)
    plan = jnp.stack([rows, tile_columns])
    group = (lax.axis_size("y"), width, local_rows)
    pieces = (devices * ROWS, LANES)

    spread = jnp.broadcast_to(start_basis.T[None], group)
    spread, first, begin, plan = lax.optimization_barrier((spread, first, begin, plan))
    gathered = gather_group(spread)
    spread, gram = call(
        first_kernel,
        [SMEM, VMEM, VMEM],
        [(group, BF16), ((width, width), F32)],
        plan, tile_values, gathered,
    )
    gathered = gather_group(spread)
    (own,) = call(
        second_kernel,
        [SMEM, VMEM, VMEM, VMEM],
        [((width, local_rows + 2 * width), F32)],
        plan, tile_values, gathered, gram,
    )
    both = of_chip(own)
    (sums,) = call(
        functools.partial(pick_kernel, nodes=local_rows, apart=apart, clusters=mine),
        [SMEM, SMEM, VMEM, VMEM],
        [(pieces, F32)],
        first, begin, seed_rows[None, :], both,
    )
    sums = sum_pieces(sums, F32, fold_kernel, ROWS)
    unit, unit_both, weights, totals = call(
        functools.partial(third_kernel, total_rows=total_rows),
        [VMEM] * 3,
        [((width, local_rows), F32), ((width, nodes), F32), ((mine, nodes), F32), ((1, nodes), F32)],
        own, both, sums,
    )
    for step in range(KSTEPS):
        if step > 0:
            weights, totals = call(
                weight_kernel, [VMEM] * 2, [((mine, nodes), F32), ((1, nodes), F32)], unit_both, centres
            )
        (sums,) = call(sum_kernel, [VMEM] * 3, [(pieces, BF16)], unit_both, weights, of_chip(totals))
        centres = sum_pieces(sums, F32, mean_kernel, PART)
    (centres,) = call(last_kernel, [VMEM], [((width, clusters), F32)], of_chip(centres))
    return unit.T, centres.T


def solution(mesh):
    sizes = (mesh.shape["group"] // 2, 2, mesh.shape["dev"] // 8, 8)
    fine = jax.sharding.Mesh(mesh.devices.reshape(sizes), ALL)
    return jax.shard_map(
        local,
        mesh=fine,
        in_specs=(P(ALL, None, None), P(ALL), P(ALL), P(ALL), P(ALL, None), P()),
        out_specs=(P(ALL, None), P()),
        check_vma=False,
    )
```

```python
import functools

import jax
import jax.numpy as jnp
from jax import lax
from jax.experimental import pallas as pl
from jax.experimental.pallas import tpu as pltpu
from jax.sharding import PartitionSpec as P

KSTEPS = 2
HI = lax.Precision.HIGHEST
F32 = jnp.float32
BF16 = jnp.bfloat16
ALL = ("z", "c", "x", "y")
GROUP = ("z",)
CHIP = "c"
DEV = ("x", "y")
LANES = 128
PART = 8
EXTRA = 2
ROWS = PART + EXTRA
GROW = 2.0**30

sharpness = 4.0


def dot(a, b, dims, precision=None):
    return lax.dot_general(a, b, (dims, ((), ())), precision=precision, preferred_element_type=F32)


def halves(x):
    high = x.astype(BF16)
    return high, (x - high.astype(F32)).astype(BF16)


def tn(a, b):
    ah, al = halves(a)
    bh, bl = halves(b)
    return dot(jnp.concatenate([ah, ah, al], axis=0), jnp.concatenate([bh, bl, bh], axis=0), ((0,), (0,)))


def nn_exact(a, b):
    ah, al = halves(a)
    both = dot(jnp.concatenate([ah, al], axis=0), b, ((1,), (0,)))
    return both[: a.shape[0]] + both[a.shape[0] :]


def cholesky(grams):
    n = grams[0].shape[0]
    blocks = n // 8
    width = 2 * n
    lane = lax.broadcasted_iota(jnp.int32, (8, n), 1)
    sub = lax.broadcasted_iota(jnp.int32, (8, n), 0)
    wide_sub = lax.broadcasted_iota(jnp.int32, (8, width), 0)
    every = [
        [
            jnp.concatenate([gram[8 * b : 8 * b + 8, :], (lane == sub + 8 * b).astype(F32)], axis=1)
            for b in range(blocks)
        ]
        for gram in grams
    ]
    for g in range(blocks):
        every_columns = [
            [
                {b: jnp.broadcast_to(rows[b][:, 8 * g + t : 8 * g + t + 1], (8, width)) for b in range(g, blocks)}
                for t in range(8)
            ]
            for rows in every
        ]
        every_pivots = [jnp.ones((8, width), F32) for _ in every]
        for t in range(8):
            for i, (rows, columns) in enumerate(zip(every, every_columns)):
                pivot = jnp.broadcast_to(columns[t][g][t : t + 1, :], (8, width))
                every_pivots[i] = jnp.where(wide_sub == t, pivot, every_pivots[i])
                inverse = 1.0 / pivot
                row = jnp.broadcast_to(rows[g][t : t + 1, :], (8, width))
                later = {m: jnp.broadcast_to(columns[m][g][t : t + 1, :], (8, width)) for m in range(t + 1, 8)}
                for b in range(g, blocks):
                    factor = columns[t][b] * inverse
                    if b == g:
                        factor = jnp.where(wide_sub > t, factor, 0.0)
                    rows[b] = rows[b] - factor * row
                    for m in range(t + 1, 8):
                        columns[m][b] = columns[m][b] - factor * later[m]
        for rows, pivots in zip(every, every_pivots):
            rows[g] = rows[g] / jnp.sqrt(pivots)
    return [jnp.concatenate(rows, axis=0) for rows in every]


def apply_tiles(plan, tiles, gathered):
    slots, block, _ = tiles.shape
    row_blocks = gathered.shape[2] // block
    left = [[] for _ in range(row_blocks)]
    for s in range(slots):
        place = plan[1, s]
        start = pl.multiple_of((place % row_blocks) * block, block)
        picked = gathered[place // row_blocks, :, pl.ds(start, block)]
        for r in range(row_blocks):
            left[r].append(jnp.where(plan[0, s] == r, picked, jnp.zeros_like(picked)))
    left = jnp.concatenate([jnp.concatenate(parts, axis=1) for parts in left], axis=0)
    right = jnp.concatenate([tiles[s] for s in range(slots)], axis=1)
    total = dot(left, right, ((1,), (1,)))
    width = gathered.shape[1]
    return jnp.concatenate([total[r * width : (r + 1) * width] for r in range(row_blocks)], axis=1)


def store_pieces(out, features, blocks):
    each = features.shape[0] // PART
    pieces = [
        piece
        for p in range(each * features.shape[1] // LANES)
        for piece in (
            features[(p % each) * PART : (p % each + 1) * PART, (p // each) * LANES : (p // each + 1) * LANES],
            blocks[p],
        )
    ]
    out[...] = jnp.concatenate(pieces, axis=0).astype(out.dtype)


def load_features(pieces, width):
    each = width // PART
    tiles = [
        jnp.concatenate([pieces[k * each + q] for q in range(each)], axis=0) for k in range(len(pieces) // each)
    ]
    return jnp.concatenate(tiles, axis=1)


def cut(array, rows):
    return [array[p : p + rows] for p in range(0, array.shape[0], rows)]


def first_kernel(plan, tiles, gathered, spread, gram):
    image = apply_tiles(plan, tiles, gathered)
    gram[...] = dot(image, image, ((1,), (1,)), HI)
    narrow = image.astype(BF16)
    for e in range(spread.shape[0]):
        spread[e] = narrow


def second_kernel(plan, tiles, gathered, gram, own):
    image = apply_tiles(plan, tiles, gathered) * GROW
    nodes = image.shape[1]
    own[:, :nodes] = image
    own[:, nodes:] = jnp.concatenate([gram[...], dot(image, image, ((1,), (1,)), HI)], axis=1)


def pick_kernel(first, begin, seeds, both, pieces, *, nodes, apart, clusters):
    chosen = seeds[:, pl.ds(pl.multiple_of(begin[0], LANES), clusters)]
    node = lax.broadcasted_iota(jnp.int32, (nodes, clusters), 0) + first[0]
    picks = sum(
        nn_exact(both[c, :, :nodes], jnp.where(chosen == node + c * apart, 1.0, 0.0).astype(BF16))
        for c in range(both.shape[0])
    )
    store_pieces(pieces, picks, cut(sum(both[c, :, nodes:] for c in range(both.shape[0])), EXTRA))


def unit_of(transform, image, total_rows):
    embedding = tn(transform, image) * jnp.sqrt(F32(total_rows))
    return embedding / jnp.sqrt(jnp.sum(embedding * embedding, axis=0, keepdims=True) + 1e-06)


def with_rows(top, first, second):
    sub = lax.broadcasted_iota(jnp.int32, (16, top.shape[1]), 0)
    return jnp.concatenate([top, jnp.where(sub == 0, first, jnp.where(sub == 1, second, 0.0))], axis=0)


def store_weights(weights, sums, unit, centres):
    square = jnp.sum(unit * unit, axis=0, keepdims=True)
    centre_square = jnp.sum(centres * centres, axis=0, keepdims=True)
    dist = tn(with_rows(-2.0 * centres, 1.0, centre_square), with_rows(unit, square, 1.0))
    value = jnp.exp(-sharpness * dist)
    weights[...] = value
    sums[...] = jnp.sum(value, axis=0, keepdims=True)


def third_kernel(own, both, received, unit_own, unit_both, weights, sums, *, total_rows):
    width, nodes = unit_own.shape
    parts = cut(received[...], ROWS)
    grams = jnp.concatenate([part[PART:] for part in parts], axis=0)
    factors, wholes = cholesky([grams[:, :width], grams[:, width:]])
    first_inverse, whole_inverse = factors[:, width:], wholes[:, width:]
    second_inverse = dot(whole_inverse, factors[:, :width], ((1,), (1,)), HI)
    transform = dot(first_inverse, second_inverse, ((0,), (1,)), HI)
    unit_own[...] = unit_of(transform, own[:, :nodes], total_rows)
    images = jnp.concatenate([both[c, :, :nodes] for c in range(both.shape[0])], axis=1)
    unit = unit_of(transform, images, total_rows)
    unit_both[...] = unit
    picks = load_features([part[:PART] for part in parts], width)
    store_weights(weights, sums, unit, unit_of(transform, picks, total_rows))


def weight_kernel(unit, received, weights, sums):
    store_weights(weights, sums, unit[...], load_features(cut(received[...], PART), unit.shape[0]))


def sum_kernel(unit, weights, sums, pieces):
    width = unit.shape[0]
    member = (weights[...] / sum(sums[c] for c in range(sums.shape[0]))).astype(BF16)
    high, low = halves(with_rows(unit[...], 1.0, 0.0))
    both = dot(jnp.concatenate([high, low], axis=0), member, ((1,), (1,)))
    total = both[: high.shape[0]] + both[high.shape[0] :]
    each = width // PART
    blocks = [
        total[width : width + EXTRA, (p // each) * LANES : (p // each + 1) * LANES]
        for p in range(pieces.shape[0] // ROWS)
    ]
    store_pieces(pieces, total[:width], blocks)


def last_kernel(received, centres):
    halves_of = [load_features(cut(received[c], PART), centres.shape[0]) for c in range(received.shape[0])]
    centres[...] = jnp.concatenate(halves_of, axis=1)


def fold_kernel(received, spread):
    total = sum(cut(received[...].astype(F32), ROWS)).astype(spread.dtype)
    spread[...] = jnp.concatenate([total] * (spread.shape[0] // ROWS), axis=0)


def mean_kernel(received, spread):
    total = sum(cut(received[...].astype(F32), ROWS))
    total = total[:PART] / total[PART : PART + 1]
    spread[...] = jnp.concatenate([total] * (spread.shape[0] // PART), axis=0)


VMEM = pl.BlockSpec(memory_space=pltpu.VMEM)
SMEM = pl.BlockSpec(memory_space=pltpu.SMEM)


def call(kernel, specs, outs, *args):
    return pl.pallas_call(
        kernel,
        in_specs=specs,
        out_specs=[VMEM] * len(outs),
        out_shape=[jax.ShapeDtypeStruct(s, d) for s, d in outs],
        compiler_params=pltpu.CompilerParams(vmem_limit_bytes=40 * 1024 * 1024),
    )(*args)


def exchange(x, axes):
    return lax.all_to_all(x, axes, 0, 0, tiled=True)


def exchange_rows(x, axes):
    together = 4 // x.dtype.itemsize
    return exchange(x.reshape(-1, together, LANES), axes).reshape(x.shape)


def gather_group(spread):
    part = exchange(spread, ("y",))
    whole = exchange(jnp.broadcast_to(part[None], (lax.axis_size("x"),) + part.shape), ("x",))
    return whole.reshape((-1,) + part.shape[1:])


def fold(kernel, x, rows, dtype):
    return call(kernel, [VMEM], [((rows, LANES), dtype)], x)[0]


def sum_pieces(pieces, middle, kernel, rows):
    mine = fold(fold_kernel, exchange_rows(pieces, DEV), ROWS * lax.axis_size(GROUP), middle)
    return exchange_rows(fold(kernel, exchange_rows(mine, GROUP), rows * lax.axis_size(DEV), F32), DEV)


def of_chip(x):
    return lax.all_gather(x, CHIP, axis=0)


def local(tile_values, tile_rows, tile_columns, tile_count, start_basis, seed_rows):
    local_rows, width = start_basis.shape
    cores, devices = lax.axis_size(CHIP), lax.axis_size(DEV)
    clusters = seed_rows.shape[0]
    mine = clusters // cores
    nodes = cores * local_rows
    total_rows = local_rows * lax.axis_size(ALL)
    apart = devices * local_rows
    first = lax.axis_index("z") * (cores * apart) + lax.axis_index(DEV) * local_rows
    first = jnp.reshape(first, (1,)).astype(jnp.int32)
    begin = jnp.reshape(lax.axis_index(CHIP) * mine, (1,)).astype(jnp.int32)
    rows = jnp.where(jnp.arange(tile_rows.shape[0], dtype=jnp.int32) < tile_count[0], tile_rows, -1)
    plan = jnp.stack([rows, tile_columns])
    group = (lax.axis_size("y"), width, local_rows)
    pieces = (devices * ROWS, LANES)

    spread = jnp.broadcast_to(start_basis.T[None], group)
    spread, first, begin, plan = lax.optimization_barrier((spread, first, begin, plan))
    gathered = gather_group(spread)
    spread, gram = call(
        first_kernel,
        [SMEM, VMEM, VMEM],
        [(group, BF16), ((width, width), F32)],
        plan, tile_values, gathered,
    )
    gathered = gather_group(spread)
    (own,) = call(
        second_kernel,
        [SMEM, VMEM, VMEM, VMEM],
        [((width, local_rows + 2 * width), F32)],
        plan, tile_values, gathered, gram,
    )
    both = of_chip(own)
    (sums,) = call(
        functools.partial(pick_kernel, nodes=local_rows, apart=apart, clusters=mine),
        [SMEM, SMEM, VMEM, VMEM],
        [(pieces, F32)],
        first, begin, seed_rows[None, :], both,
    )
    sums = sum_pieces(sums, F32, fold_kernel, ROWS)
    unit, unit_both, weights, totals = call(
        functools.partial(third_kernel, total_rows=total_rows),
        [VMEM] * 3,
        [((width, local_rows), F32), ((width, nodes), F32), ((mine, nodes), F32), ((1, nodes), F32)],
        own, both, sums,
    )
    for step in range(KSTEPS):
        if step > 0:
            weights, totals = call(
                weight_kernel, [VMEM] * 2, [((mine, nodes), F32), ((1, nodes), F32)], unit_both, centres
            )
        (sums,) = call(sum_kernel, [VMEM] * 3, [(pieces, BF16)], unit_both, weights, of_chip(totals))
        centres = sum_pieces(sums, F32, mean_kernel, PART)
    (centres,) = call(last_kernel, [VMEM], [((width, clusters), F32)], of_chip(centres))
    return unit.T, centres.T


def solution(mesh):
    sizes = (mesh.shape["group"] // 2, 2, mesh.shape["dev"] // 8, 8)
    fine = jax.sharding.Mesh(mesh.devices.reshape(sizes), ALL)
    return jax.shard_map(
        local,
        mesh=fine,
        in_specs=(P(ALL, None, None), P(ALL), P(ALL), P(ALL), P(ALL, None), P()),
        out_specs=(P(ALL, None), P()),
        check_vma=False,
    )
```

```python
import functools

import jax
import jax.numpy as jnp
from jax import lax
from jax.experimental import pallas as pl
from jax.experimental.pallas import tpu as pltpu
from jax.sharding import PartitionSpec as P

KSTEPS = 2
HI = lax.Precision.HIGHEST
F32 = jnp.float32
BF16 = jnp.bfloat16
ALL = ("z", "c", "x", "y")
GROUP = ("z",)
CHIP = "c"
DEV = ("x", "y")
LANES = 128
PART = 8
EXTRA = 2
ROWS = PART + EXTRA
GROW = 2.0**30
COLUMN_BITS = 6
COLUMNS = 2**COLUMN_BITS

sharpness = 4.0


def dot(a, b, dims, precision=None):
    return lax.dot_general(a, b, (dims, ((), ())), precision=precision, preferred_element_type=F32)


def halves(x):
    high = x.astype(BF16)
    return high, (x - high.astype(F32)).astype(BF16)


def tn(a, b):
    ah, al = halves(a)
    bh, bl = halves(b)
    return dot(jnp.concatenate([ah, ah, al], axis=0), jnp.concatenate([bh, bl, bh], axis=0), ((0,), (0,)))


def nn_exact(a, b):
    ah, al = halves(a)
    both = dot(jnp.concatenate([ah, al], axis=0), b, ((1,), (0,)))
    return both[: a.shape[0]] + both[a.shape[0] :]


def cholesky(grams):
    n = grams[0].shape[0]
    blocks = n // 8
    width = 2 * n
    lane = lax.broadcasted_iota(jnp.int32, (8, n), 1)
    sub = lax.broadcasted_iota(jnp.int32, (8, n), 0)
    wide_sub = lax.broadcasted_iota(jnp.int32, (8, width), 0)
    every = [
        [
            jnp.concatenate([gram[8 * b : 8 * b + 8, :], (lane == sub + 8 * b).astype(F32)], axis=1)
            for b in range(blocks)
        ]
        for gram in grams
    ]
    for g in range(blocks):
        every_columns = [
            [
                {b: jnp.broadcast_to(rows[b][:, 8 * g + t : 8 * g + t + 1], (8, width)) for b in range(g, blocks)}
                for t in range(8)
            ]
            for rows in every
        ]
        every_pivots = [jnp.ones((8, width), F32) for _ in every]
        for t in range(8):
            for i, (rows, columns) in enumerate(zip(every, every_columns)):
                pivot = jnp.broadcast_to(columns[t][g][t : t + 1, :], (8, width))
                every_pivots[i] = jnp.where(wide_sub == t, pivot, every_pivots[i])
                inverse = 1.0 / pivot
                row = jnp.broadcast_to(rows[g][t : t + 1, :], (8, width))
                later = {m: jnp.broadcast_to(columns[m][g][t : t + 1, :], (8, width)) for m in range(t + 1, 8)}
                for b in range(g, blocks):
                    factor = columns[t][b] * inverse
                    if b == g:
                        factor = jnp.where(wide_sub > t, factor, 0.0)
                    rows[b] = rows[b] - factor * row
                    for m in range(t + 1, 8):
                        columns[m][b] = columns[m][b] - factor * later[m]
        for rows, pivots in zip(every, every_pivots):
            rows[g] = rows[g] / jnp.sqrt(pivots)
    return [jnp.concatenate(rows, axis=0) for rows in every]


def apply_tiles(plan, tiles, gathered):
    slots, block, _ = tiles.shape
    row_blocks = gathered.shape[2] // block
    left = [[] for _ in range(row_blocks)]
    for s in range(slots):
        place = plan[s] & (COLUMNS - 1)
        start = pl.multiple_of((place % row_blocks) * block, block)
        picked = gathered[place // row_blocks, :, pl.ds(start, block)]
        for r in range(row_blocks):
            left[r].append(jnp.where(plan[s] >> COLUMN_BITS == r, picked, jnp.zeros_like(picked)))
    left = jnp.concatenate([jnp.concatenate(parts, axis=1) for parts in left], axis=0)
    right = jnp.concatenate([tiles[s] for s in range(slots)], axis=1)
    total = dot(left, right, ((1,), (1,)))
    width = gathered.shape[1]
    return jnp.concatenate([total[r * width : (r + 1) * width] for r in range(row_blocks)], axis=1)


def store_pieces(out, features, blocks):
    each = features.shape[0] // PART
    pieces = [
        piece
        for p in range(each * features.shape[1] // LANES)
        for piece in (
            features[(p % each) * PART : (p % each + 1) * PART, (p // each) * LANES : (p // each + 1) * LANES],
            blocks[p],
        )
    ]
    out[...] = jnp.concatenate(pieces, axis=0).astype(out.dtype)


def load_features(pieces, width):
    each = width // PART
    tiles = [
        jnp.concatenate([pieces[k * each + q] for q in range(each)], axis=0) for k in range(len(pieces) // each)
    ]
    return jnp.concatenate(tiles, axis=1)


def cut(array, rows):
    return [array[p : p + rows] for p in range(0, array.shape[0], rows)]


def first_kernel(plan, tiles, gathered, spread, gram):
    image = apply_tiles(plan, tiles, gathered)
    gram[...] = dot(image, image, ((1,), (1,)), HI)
    narrow = image.astype(BF16)
    for e in range(spread.shape[0]):
        spread[e] = narrow


def second_kernel(plan, tiles, gathered, gram, own):
    image = apply_tiles(plan, tiles, gathered) * GROW
    nodes = image.shape[1]
    own[:, :nodes] = image
    own[:, nodes:] = jnp.concatenate([gram[...], dot(image, image, ((1,), (1,)), HI)], axis=1)


def pick_kernel(first, begin, seeds, both, pieces, *, nodes, apart, clusters):
    chosen = seeds[:, pl.ds(pl.multiple_of(begin[0], LANES), clusters)]
    node = lax.broadcasted_iota(jnp.int32, (nodes, clusters), 0) + first[0]
    picks = sum(
        nn_exact(both[c, :, :nodes], jnp.where(chosen == node + c * apart, 1.0, 0.0).astype(BF16))
        for c in range(both.shape[0])
    )
    store_pieces(pieces, picks, cut(sum(both[c, :, nodes:] for c in range(both.shape[0])), EXTRA))


def unit_of(transform, image, total_rows):
    embedding = tn(transform, image) * jnp.sqrt(F32(total_rows))
    return embedding / jnp.sqrt(jnp.sum(embedding * embedding, axis=0, keepdims=True) + 1e-06)


def with_rows(top, first, second):
    sub = lax.broadcasted_iota(jnp.int32, (16, top.shape[1]), 0)
    return jnp.concatenate([top, jnp.where(sub == 0, first, jnp.where(sub == 1, second, 0.0))], axis=0)


def store_weights(weights, sums, unit, centres):
    square = jnp.sum(unit * unit, axis=0, keepdims=True)
    centre_square = jnp.sum(centres * centres, axis=0, keepdims=True)
    dist = tn(with_rows(-2.0 * centres, 1.0, centre_square), with_rows(unit, square, 1.0))
    value = jnp.exp(-sharpness * dist)
    weights[...] = value
    sums[...] = jnp.sum(value, axis=0, keepdims=True)


def third_kernel(own, both, received, unit_own, unit_both, weights, sums, *, total_rows):
    width, nodes = unit_own.shape
    parts = cut(received[...], ROWS)
    grams = jnp.concatenate([part[PART:] for part in parts], axis=0)
    factors, wholes = cholesky([grams[:, :width], grams[:, width:]])
    first_inverse, whole_inverse = factors[:, width:], wholes[:, width:]
    second_inverse = dot(whole_inverse, factors[:, :width], ((1,), (1,)), HI)
    transform = dot(first_inverse, second_inverse, ((0,), (1,)), HI)
    unit_own[...] = unit_of(transform, own[:, :nodes], total_rows)
    images = jnp.concatenate([both[c, :, :nodes] for c in range(both.shape[0])], axis=1)
    unit = unit_of(transform, images, total_rows)
    unit_both[...] = unit
    picks = load_features([part[:PART] for part in parts], width)
    store_weights(weights, sums, unit, unit_of(transform, picks, total_rows))


def weight_kernel(unit, received, weights, sums):
    store_weights(weights, sums, unit[...], load_features(cut(received[...], PART), unit.shape[0]))


def sum_kernel(unit, weights, sums, pieces):
    width = unit.shape[0]
    member = (weights[...] / sum(sums[c] for c in range(sums.shape[0]))).astype(BF16)
    high, low = halves(with_rows(unit[...], 1.0, 0.0))
    both = dot(jnp.concatenate([high, low], axis=0), member, ((1,), (1,)))
    total = both[: high.shape[0]] + both[high.shape[0] :]
    each = width // PART
    blocks = [
        total[width : width + EXTRA, (p // each) * LANES : (p // each + 1) * LANES]
        for p in range(pieces.shape[0] // ROWS)
    ]
    store_pieces(pieces, total[:width], blocks)


def last_kernel(received, centres):
    halves_of = [load_features(cut(received[c], PART), centres.shape[0]) for c in range(received.shape[0])]
    centres[...] = jnp.concatenate(halves_of, axis=1)


def fold_kernel(received, spread):
    total = sum(cut(received[...].astype(F32), ROWS)).astype(spread.dtype)
    spread[...] = jnp.concatenate([total] * (spread.shape[0] // ROWS), axis=0)


def mean_kernel(received, spread):
    total = sum(cut(received[...].astype(F32), ROWS))
    total = total[:PART] / total[PART : PART + 1]
    spread[...] = jnp.concatenate([total] * (spread.shape[0] // PART), axis=0)


VMEM = pl.BlockSpec(memory_space=pltpu.VMEM)
SMEM = pl.BlockSpec(memory_space=pltpu.SMEM)


def call(kernel, specs, outs, *args):
    return pl.pallas_call(
        kernel,
        in_specs=specs,
        out_specs=[VMEM] * len(outs),
        out_shape=[jax.ShapeDtypeStruct(s, d) for s, d in outs],
        compiler_params=pltpu.CompilerParams(vmem_limit_bytes=40 * 1024 * 1024),
    )(*args)


def exchange(x, axes):
    return lax.all_to_all(x, axes, 0, 0, tiled=True)


def exchange_rows(x, axes):
    together = 4 // x.dtype.itemsize
    return exchange(x.reshape(-1, together, LANES), axes).reshape(x.shape)


def gather_group(spread):
    part = exchange(spread, ("y",))
    whole = exchange(jnp.broadcast_to(part[None], (lax.axis_size("x"),) + part.shape), ("x",))
    return whole.reshape((-1,) + part.shape[1:])


def fold(kernel, x, rows, dtype):
    return call(kernel, [VMEM], [((rows, LANES), dtype)], x)[0]


def sum_pieces(pieces, middle, kernel, rows):
    mine = fold(fold_kernel, exchange_rows(pieces, DEV), ROWS * lax.axis_size(GROUP), middle)
    return exchange_rows(fold(kernel, exchange_rows(mine, GROUP), rows * lax.axis_size(DEV), F32), DEV)


def of_chip(x):
    return lax.all_gather(x, CHIP, axis=0)


def local(tile_values, tile_rows, tile_columns, tile_count, start_basis, seed_rows):
    local_rows, width = start_basis.shape
    cores, devices = lax.axis_size(CHIP), lax.axis_size(DEV)
    clusters = seed_rows.shape[0]
    mine = clusters // cores
    nodes = cores * local_rows
    total_rows = local_rows * lax.axis_size(ALL)
    apart = devices * local_rows
    first = lax.axis_index("z") * (cores * apart) + lax.axis_index(DEV) * local_rows
    first = jnp.reshape(first, (1,)).astype(jnp.int32)
    begin = jnp.reshape(lax.axis_index(CHIP) * mine, (1,)).astype(jnp.int32)
    live = jnp.arange(tile_rows.shape[0], dtype=jnp.int32) < tile_count[0]
    plan = jnp.where(live, tile_rows * COLUMNS + tile_columns, -1)
    group = (lax.axis_size("y"), width, local_rows)
    pieces = (devices * ROWS, LANES)

    spread = jnp.broadcast_to(start_basis.T[None], group)
    spread, first, begin, plan = lax.optimization_barrier((spread, first, begin, plan))
    gathered = gather_group(spread)
    spread, gram = call(
        first_kernel,
        [SMEM, VMEM, VMEM],
        [(group, BF16), ((width, width), F32)],
        plan, tile_values, gathered,
    )
    gathered = gather_group(spread)
    (own,) = call(
        second_kernel,
        [SMEM, VMEM, VMEM, VMEM],
        [((width, local_rows + 2 * width), F32)],
        plan, tile_values, gathered, gram,
    )
    both = of_chip(own)
    (sums,) = call(
        functools.partial(pick_kernel, nodes=local_rows, apart=apart, clusters=mine),
        [SMEM, SMEM, VMEM, VMEM],
        [(pieces, F32)],
        first, begin, seed_rows[None, :], both,
    )
    sums = sum_pieces(sums, F32, fold_kernel, ROWS)
    unit, unit_both, weights, totals = call(
        functools.partial(third_kernel, total_rows=total_rows),
        [VMEM] * 3,
        [((width, local_rows), F32), ((width, nodes), F32), ((mine, nodes), F32), ((1, nodes), F32)],
        own, both, sums,
    )
    for step in range(KSTEPS):
        if step > 0:
            weights, totals = call(
                weight_kernel, [VMEM] * 2, [((mine, nodes), F32), ((1, nodes), F32)], unit_both, centres
            )
        (sums,) = call(sum_kernel, [VMEM] * 3, [(pieces, BF16)], unit_both, weights, of_chip(totals))
        centres = sum_pieces(sums, F32, mean_kernel, PART)
    (centres,) = call(last_kernel, [VMEM], [((width, clusters), F32)], of_chip(centres))
    return unit.T, centres.T


def solution(mesh):
    sizes = (mesh.shape["group"] // 2, 2, mesh.shape["dev"] // 8, 8)
    fine = jax.sharding.Mesh(mesh.devices.reshape(sizes), ALL)
    return jax.shard_map(
        local,
        mesh=fine,
        in_specs=(P(ALL, None, None), P(ALL), P(ALL), P(ALL), P(ALL, None), P()),
        out_specs=(P(ALL, None), P()),
        check_vma=False,
    )
```

```python
import functools

import jax
import jax.numpy as jnp
from jax import lax
from jax.experimental import pallas as pl
from jax.experimental.pallas import tpu as pltpu
from jax.sharding import PartitionSpec as P

KSTEPS = 2
HI = lax.Precision.HIGHEST
F32 = jnp.float32
BF16 = jnp.bfloat16
ALL = ("z", "c", "x", "y")
GROUP = ("z",)
CHIP = "c"
DEV = ("x", "y")
LANES = 128
PART = 8
EXTRA = 2
ROWS = PART + EXTRA
GROW = 2.0**30
COLUMN_BITS = 6
COLUMNS = 2**COLUMN_BITS

sharpness = 4.0


def dot(a, b, dims, precision=None):
    return lax.dot_general(a, b, (dims, ((), ())), precision=precision, preferred_element_type=F32)


def halves(x):
    high = x.astype(BF16)
    return high, (x - high.astype(F32)).astype(BF16)


def tn(a, b):
    ah, al = halves(a)
    bh, bl = halves(b)
    return dot(jnp.concatenate([ah, ah, al], axis=0), jnp.concatenate([bh, bl, bh], axis=0), ((0,), (0,)))


def gram_of(a):
    high, low = halves(a)
    left, right = jnp.concatenate([high, high, low], axis=1), jnp.concatenate([high, low, high], axis=1)
    return dot(left, right, ((1,), (1,)))


def nn_exact(a, b):
    ah, al = halves(a)
    both = dot(jnp.concatenate([ah, al], axis=0), b, ((1,), (0,)))
    return both[: a.shape[0]] + both[a.shape[0] :]


def cholesky(grams):
    n = grams[0].shape[0]
    blocks = n // 8
    width = 2 * n
    lane = lax.broadcasted_iota(jnp.int32, (8, n), 1)
    sub = lax.broadcasted_iota(jnp.int32, (8, n), 0)
    wide_sub = lax.broadcasted_iota(jnp.int32, (8, width), 0)
    every = [
        [
            jnp.concatenate([gram[8 * b : 8 * b + 8, :], (lane == sub + 8 * b).astype(F32)], axis=1)
            for b in range(blocks)
        ]
        for gram in grams
    ]
    for g in range(blocks):
        every_columns = [
            [
                {b: jnp.broadcast_to(rows[b][:, 8 * g + t : 8 * g + t + 1], (8, width)) for b in range(g, blocks)}
                for t in range(8)
            ]
            for rows in every
        ]
        every_pivots = [jnp.ones((8, width), F32) for _ in every]
        for t in range(8):
            for i, (rows, columns) in enumerate(zip(every, every_columns)):
                pivot = jnp.broadcast_to(columns[t][g][t : t + 1, :], (8, width))
                every_pivots[i] = jnp.where(wide_sub == t, pivot, every_pivots[i])
                inverse = 1.0 / pivot
                row = jnp.broadcast_to(rows[g][t : t + 1, :], (8, width))
                later = {m: jnp.broadcast_to(columns[m][g][t : t + 1, :], (8, width)) for m in range(t + 1, 8)}
                for b in range(g, blocks):
                    factor = columns[t][b] * inverse
                    if b == g:
                        factor = jnp.where(wide_sub > t, factor, 0.0)
                    rows[b] = rows[b] - factor * row
                    for m in range(t + 1, 8):
                        columns[m][b] = columns[m][b] - factor * later[m]
        for rows, pivots in zip(every, every_pivots):
            rows[g] = rows[g] / jnp.sqrt(pivots)
    return [jnp.concatenate(rows, axis=0) for rows in every]


def apply_tiles(plan, tiles, gathered):
    slots, block, _ = tiles.shape
    row_blocks = gathered.shape[2] // block
    left = [[] for _ in range(row_blocks)]
    for s in range(slots):
        place = plan[s] & (COLUMNS - 1)
        start = pl.multiple_of((place % row_blocks) * block, block)
        picked = gathered[place // row_blocks, :, pl.ds(start, block)]
        for r in range(row_blocks):
            left[r].append(jnp.where(plan[s] >> COLUMN_BITS == r, picked, jnp.zeros_like(picked)))
    left = jnp.concatenate([jnp.concatenate(parts, axis=1) for parts in left], axis=0)
    right = jnp.concatenate([tiles[s] for s in range(slots)], axis=1)
    total = dot(left, right, ((1,), (1,)))
    width = gathered.shape[1]
    return jnp.concatenate([total[r * width : (r + 1) * width] for r in range(row_blocks)], axis=1)


def store_pieces(out, features, blocks):
    each = features.shape[0] // PART
    pieces = [
        piece
        for p in range(each * features.shape[1] // LANES)
        for piece in (
            features[(p % each) * PART : (p % each + 1) * PART, (p // each) * LANES : (p // each + 1) * LANES],
            blocks[p],
        )
    ]
    out[...] = jnp.concatenate(pieces, axis=0).astype(out.dtype)


def load_features(pieces, width):
    each = width // PART
    tiles = [
        jnp.concatenate([pieces[k * each + q] for q in range(each)], axis=0) for k in range(len(pieces) // each)
    ]
    return jnp.concatenate(tiles, axis=1)


def cut(array, rows):
    return [array[p : p + rows] for p in range(0, array.shape[0], rows)]


def first_kernel(plan, tiles, gathered, spread, gram):
    image = apply_tiles(plan, tiles, gathered)
    gram[...] = gram_of(image)
    narrow = image.astype(BF16)
    for e in range(spread.shape[0]):
        spread[e] = narrow


def second_kernel(plan, tiles, gathered, gram, own):
    image = apply_tiles(plan, tiles, gathered) * GROW
    nodes = image.shape[1]
    own[:, :nodes] = image
    own[:, nodes:] = jnp.concatenate([gram[...], gram_of(image)], axis=1)


def pick_kernel(first, begin, seeds, both, pieces, *, nodes, apart, clusters):
    chosen = seeds[:, pl.ds(pl.multiple_of(begin[0], LANES), clusters)]
    node = lax.broadcasted_iota(jnp.int32, (nodes, clusters), 0) + first[0]
    picks = sum(
        nn_exact(both[c, :, :nodes], jnp.where(chosen == node + c * apart, 1.0, 0.0).astype(BF16))
        for c in range(both.shape[0])
    )
    store_pieces(pieces, picks, cut(sum(both[c, :, nodes:] for c in range(both.shape[0])), EXTRA))


def unit_of(transform, image, total_rows):
    embedding = tn(transform, image) * jnp.sqrt(F32(total_rows))
    return embedding / jnp.sqrt(jnp.sum(embedding * embedding, axis=0, keepdims=True) + 1e-06)


def with_rows(top, first, second):
    sub = lax.broadcasted_iota(jnp.int32, (16, top.shape[1]), 0)
    return jnp.concatenate([top, jnp.where(sub == 0, first, jnp.where(sub == 1, second, 0.0))], axis=0)


def store_weights(weights, sums, unit, centres):
    square = jnp.sum(unit * unit, axis=0, keepdims=True)
    centre_square = jnp.sum(centres * centres, axis=0, keepdims=True)
    dist = tn(with_rows(-2.0 * centres, 1.0, centre_square), with_rows(unit, square, 1.0))
    value = jnp.exp(-sharpness * dist)
    weights[...] = value
    sums[...] = jnp.sum(value, axis=0, keepdims=True)


def third_kernel(own, both, received, unit_own, unit_both, weights, sums, *, total_rows):
    width, nodes = unit_own.shape
    parts = cut(received[...], ROWS)
    grams = jnp.concatenate([part[PART:] for part in parts], axis=0)
    factors, wholes = cholesky([grams[:, :width], grams[:, width:]])
    first_inverse, whole_inverse = factors[:, width:], wholes[:, width:]
    second_inverse = dot(whole_inverse, factors[:, :width], ((1,), (1,)), HI)
    transform = dot(first_inverse, second_inverse, ((0,), (1,)), HI)
    unit_own[...] = unit_of(transform, own[:, :nodes], total_rows)
    images = jnp.concatenate([both[c, :, :nodes] for c in range(both.shape[0])], axis=1)
    unit = unit_of(transform, images, total_rows)
    unit_both[...] = unit
    picks = load_features([part[:PART] for part in parts], width)
    store_weights(weights, sums, unit, unit_of(transform, picks, total_rows))


def weight_kernel(unit, received, weights, sums):
    store_weights(weights, sums, unit[...], load_features(cut(received[...], PART), unit.shape[0]))


def sum_kernel(unit, weights, sums, pieces):
    width = unit.shape[0]
    member = (weights[...] / sum(sums[c] for c in range(sums.shape[0]))).astype(BF16)
    high, low = halves(with_rows(unit[...], 1.0, 0.0))
    both = dot(jnp.concatenate([high, low], axis=0), member, ((1,), (1,)))
    total = both[: high.shape[0]] + both[high.shape[0] :]
    each = width // PART
    blocks = [
        total[width : width + EXTRA, (p // each) * LANES : (p // each + 1) * LANES]
        for p in range(pieces.shape[0] // ROWS)
    ]
    store_pieces(pieces, total[:width], blocks)


def last_kernel(received, centres):
    halves_of = [load_features(cut(received[c], PART), centres.shape[0]) for c in range(received.shape[0])]
    centres[...] = jnp.concatenate(halves_of, axis=1)


def fold_kernel(received, spread):
    total = sum(cut(received[...].astype(F32), ROWS)).astype(spread.dtype)
    spread[...] = jnp.concatenate([total] * (spread.shape[0] // ROWS), axis=0)


def mean_kernel(received, spread):
    total = sum(cut(received[...].astype(F32), ROWS))
    total = total[:PART] / total[PART : PART + 1]
    spread[...] = jnp.concatenate([total] * (spread.shape[0] // PART), axis=0)


VMEM = pl.BlockSpec(memory_space=pltpu.VMEM)
SMEM = pl.BlockSpec(memory_space=pltpu.SMEM)


def call(kernel, specs, outs, *args):
    return pl.pallas_call(
        kernel,
        in_specs=specs,
        out_specs=[VMEM] * len(outs),
        out_shape=[jax.ShapeDtypeStruct(s, d) for s, d in outs],
        compiler_params=pltpu.CompilerParams(vmem_limit_bytes=40 * 1024 * 1024),
    )(*args)


def exchange(x, axes):
    return lax.all_to_all(x, axes, 0, 0, tiled=True)


def exchange_rows(x, axes):
    together = 4 // x.dtype.itemsize
    return exchange(x.reshape(-1, together, LANES), axes).reshape(x.shape)


def gather_group(spread):
    part = exchange(spread, ("y",))
    whole = exchange(jnp.broadcast_to(part[None], (lax.axis_size("x"),) + part.shape), ("x",))
    return whole.reshape((-1,) + part.shape[1:])


def fold(kernel, x, rows, dtype):
    return call(kernel, [VMEM], [((rows, LANES), dtype)], x)[0]


def sum_pieces(pieces, middle, kernel, rows):
    mine = fold(fold_kernel, exchange_rows(pieces, DEV), ROWS * lax.axis_size(GROUP), middle)
    return exchange_rows(fold(kernel, exchange_rows(mine, GROUP), rows * lax.axis_size(DEV), F32), DEV)


def of_chip(x):
    return lax.all_gather(x, CHIP, axis=0)


def local(tile_values, tile_rows, tile_columns, tile_count, start_basis, seed_rows):
    local_rows, width = start_basis.shape
    cores, devices = lax.axis_size(CHIP), lax.axis_size(DEV)
    clusters = seed_rows.shape[0]
    mine = clusters // cores
    nodes = cores * local_rows
    total_rows = local_rows * lax.axis_size(ALL)
    apart = devices * local_rows
    first = lax.axis_index("z") * (cores * apart) + lax.axis_index(DEV) * local_rows
    first = jnp.reshape(first, (1,)).astype(jnp.int32)
    begin = jnp.reshape(lax.axis_index(CHIP) * mine, (1,)).astype(jnp.int32)
    live = jnp.arange(tile_rows.shape[0], dtype=jnp.int32) < tile_count[0]
    plan = jnp.where(live, tile_rows * COLUMNS + tile_columns, -1)
    group = (lax.axis_size("y"), width, local_rows)
    pieces = (devices * ROWS, LANES)

    spread = jnp.broadcast_to(start_basis.T[None], group)
    spread, first, begin, plan = lax.optimization_barrier((spread, first, begin, plan))
    gathered = gather_group(spread)
    spread, gram = call(
        first_kernel,
        [SMEM, VMEM, VMEM],
        [(group, BF16), ((width, width), F32)],
        plan, tile_values, gathered,
    )
    gathered = gather_group(spread)
    (own,) = call(
        second_kernel,
        [SMEM, VMEM, VMEM, VMEM],
        [((width, local_rows + 2 * width), F32)],
        plan, tile_values, gathered, gram,
    )
    both = of_chip(own)
    (sums,) = call(
        functools.partial(pick_kernel, nodes=local_rows, apart=apart, clusters=mine),
        [SMEM, SMEM, VMEM, VMEM],
        [(pieces, F32)],
        first, begin, seed_rows[None, :], both,
    )
    sums = sum_pieces(sums, F32, fold_kernel, ROWS)
    unit, unit_both, weights, totals = call(
        functools.partial(third_kernel, total_rows=total_rows),
        [VMEM] * 3,
        [((width, local_rows), F32), ((width, nodes), F32), ((mine, nodes), F32), ((1, nodes), F32)],
        own, both, sums,
    )
    for step in range(KSTEPS):
        if step > 0:
            weights, totals = call(
                weight_kernel, [VMEM] * 2, [((mine, nodes), F32), ((1, nodes), F32)], unit_both, centres
            )
        (sums,) = call(sum_kernel, [VMEM] * 3, [(pieces, BF16)], unit_both, weights, of_chip(totals))
        centres = sum_pieces(sums, F32, mean_kernel, PART)
    (centres,) = call(last_kernel, [VMEM], [((width, clusters), F32)], of_chip(centres))
    return unit.T, centres.T


def solution(mesh):
    sizes = (mesh.shape["group"] // 2, 2, mesh.shape["dev"] // 8, 8)
    fine = jax.sharding.Mesh(mesh.devices.reshape(sizes), ALL)
    return jax.shard_map(
        local,
        mesh=fine,
        in_specs=(P(ALL, None, None), P(ALL), P(ALL), P(ALL), P(ALL, None), P()),
        out_specs=(P(ALL, None), P()),
        check_vma=False,
    )
```
